256 devices in a mesh: wide: 16 (over z_hi, y, core), tp: 4 (over z_lo), prompt: 4 (over x).
Axes of the slice: x: 4, y: 4, z: 8 (z_hi: 2, z_lo: 4; z = z_hi * 4 + z_lo), core: 2. Of those that a mesh axis runs over, the one named last changes fastest.
Arguments:
- span_query: bfloat16 [32768, 16, 128], P(('prompt', 'wide'), 'tp'), parts along dimension 0, may hold values from -6 to 6
- span_key: bfloat16 [32768, 16, 128], P(('prompt', 'wide'), 'tp'), parts along dimension 0, may hold values from -6 to 6
- span_value: bfloat16 [32768, 32, 128], P(('prompt', 'wide'), 'tp'), parts along dimension 0, may hold values from -6 to 6
- span_beta_logit: float32 [32768, 32], P(('prompt', 'wide'), 'tp'), parts along dimension 0, may hold values from -5 to -2
- span_logdecay: float32 [32768, 32], P(('prompt', 'wide'), 'tp'), parts along dimension 0, may hold values from -0.8 to 0
- span_gate: bfloat16 [32768, 32, 128], P(('prompt', 'wide'), 'tp'), parts along dimension 0, may hold values from -6 to 6
- norm_gain: float32 [128], replicated, may hold values from 0.1 to 1.9
- prior_state: float32 [128, 128, 128], P(('prompt', 'tp')), parts along dimension 0, may hold values from -1.25 to 1.25
- step_query: bfloat16 [64, 4, 16, 128], P(('prompt', 'wide'), None, 'tp'), parts along dimension 0, may hold values from -6 to 6
- step_key: bfloat16 [64, 4, 16, 128], P(('prompt', 'wide'), None, 'tp'), parts along dimension 0, may hold values from -6 to 6
- step_value: bfloat16 [64, 4, 32, 128], P(('prompt', 'wide'), None, 'tp'), parts along dimension 0, may hold values from -6 to 6
- step_beta_logit: float32 [64, 4, 32], P(('prompt', 'wide'), None, 'tp'), parts along dimension 0, may hold values from -2 to 1
- step_logdecay: float32 [64, 4, 32], P(('prompt', 'wide'), None, 'tp'), parts along dimension 0, may hold values from -0.7 to -0.02
- step_gate: bfloat16 [64, 4, 32, 128], P(('prompt', 'wide'), None, 'tp'), parts along dimension 0, may hold values from -6 to 6
- cache_key: bfloat16 [131072, 2, 256], P(('prompt', 'wide')), parts along dimension 0, may hold values from -6 to 6
- cache_value: bfloat16 [131072, 2, 256], P(('prompt', 'wide')), parts along dimension 0, may hold values from -6 to 6
- att_query: bfloat16 [64, 4, 16, 256], P(('prompt', 'wide'), None, 'tp'), parts along dimension 0, may hold values from -6 to 6
- att_key: bfloat16 [64, 4, 2, 256], P(('prompt', 'wide')), parts along dimension 0, may hold values from -6 to 6
- att_value: bfloat16 [64, 4, 2, 256], P(('prompt', 'wide')), parts along dimension 0, may hold values from -6 to 6
- att_gate: bfloat16 [64, 4, 16, 256], P(('prompt', 'wide'), None, 'tp'), parts along dimension 0, may hold values from -6 to 6
Outputs:
- span_out: bfloat16 [32768, 4096], P(('prompt', 'wide'), 'tp'), parts along dimension 0
- step_out: bfloat16 [64, 4, 4096], P(('prompt', 'wide'), None, 'tp'), parts along dimension 0
- final_state: float32 [64, 32, 128, 128], P(('prompt', 'wide'), 'tp'), parts along dimension 0
- att_out: bfloat16 [64, 4, 4096], P(('prompt', 'wide'), None, 'tp'), parts along dimension 0
The draws below stay inside these ranges and needn't reach their ends.
There are 4 independent parts, one for each index of `prompt`. The reference program is written for one: setup_inputs(seed, part) draws one part's arguments, and reference() takes and returns one part's arrays. A program takes and returns all parts, laid end to end along the dimension named above; an argument that names none is the same for every part. Nothing has to cross between parts.
All inputs are finite; a program needn't handle non-finite values.
Results may differ from the reference program's by a relative error of at most 0.0044.
Values may be sent and summed in bfloat16 or wider, within the bound.
A program may use at most 128 MiB of HBM per device.

```python
import math
import jax
import jax.numpy as jnp
from jax import lax

HK = 16
VALUE_HEADS = 32
DK = 128
DV = 128
QH = 16
KVH = 2
HD = 256
STEPS = 4
SPAN_TOKENS = 8192
CTX = 32768
SAMPLES = 16


def draw_span_logdecay(key, part):
    random_subkeys = jax.random.split(jax.random.fold_in(key, 5), 6)
    slow_share = 0.5
    chooser = jax.random.uniform(random_subkeys[0], (VALUE_HEADS,))
    slow_rate = jnp.exp(jax.random.uniform(random_subkeys[1], (VALUE_HEADS,), minval=math.log(0.05), maxval=math.log(0.3))) / SPAN_TOKENS
    fast_rate = jnp.exp(jax.random.uniform(random_subkeys[2], (VALUE_HEADS,), minval=math.log(1.0 / 50.0), maxval=math.log(1.0 / 30.0)))
    per_head_rate = jnp.where(chooser < slow_share, slow_rate, fast_rate)
    random_noise = jnp.exp(jax.random.uniform(random_subkeys[3], (SPAN_TOKENS, VALUE_HEADS), minval=math.log(0.5), maxval=math.log(2.0)))
    spike_token_positions = jax.random.randint(random_subkeys[4], (2,), 0, SPAN_TOKENS)
    token_positions = jnp.arange(SPAN_TOKENS)
    spike_events = jnp.any(token_positions[:, None] == spike_token_positions[None, :], axis=1).astype(jnp.float32)
    spike_loss_term = jax.random.uniform(random_subkeys[5], (VALUE_HEADS,), minval=0.22, maxval=0.69)
    return -(per_head_rate[None, :] * random_noise) - spike_events[:, None] * spike_loss_term[None, :]


def draw_span_key(key, part):
    random_subkeys = jax.random.split(jax.random.fold_in(key, 23), 1)
    noise_part = jax.random.normal(random_subkeys[0], (SPAN_TOKENS, HK, DK), jnp.float32)
    return jnp.clip(noise_part, -6.0, 6.0).astype(jnp.bfloat16)


def attention_parts(key):
    random_subkeys = jax.random.split(jax.random.fold_in(key, 17), 3)
    cache_rows = jnp.clip(jax.random.normal(random_subkeys[0], (CTX, KVH, HD), jnp.float32), -6.0, 6.0)
    query_vectors = jnp.clip(jax.random.normal(random_subkeys[1], (SAMPLES, STEPS, QH, HD), jnp.float32), -6.0, 6.0)
    jitter_own = jax.random.normal(random_subkeys[2], (SAMPLES, STEPS, KVH, HD), jnp.float32)
    grouped = jnp.sum(query_vectors.reshape(SAMPLES, STEPS, KVH, QH // KVH, HD), axis=3) / math.sqrt(QH // KVH)
    own_keys = jnp.clip(1.6 * grouped + 0.6 * jitter_own, -6.0, 6.0)
    return (cache_rows, query_vectors, own_keys)


def draw_cache_key(key, part):
    return attention_parts(key)[0].astype(jnp.bfloat16)


def draw_att_query(key, part):
    return attention_parts(key)[1].astype(jnp.bfloat16)


def draw_att_key(key, part):
    return attention_parts(key)[2].astype(jnp.bfloat16)


def block_scale(key, shape, cuts, least, high):
    loudness = 1.0
    for position, parts in cuts:
        draws = jax.random.uniform(jax.random.fold_in(jax.random.fold_in(key, 6), position), (parts,), jnp.float32, least / len(cuts), high / len(cuts))
        loudness = loudness * jnp.repeat(jnp.exp(draws), shape[position] // parts).reshape((-1,) + (1,) * (len(shape) - 1 - position))
    return loudness


def noise(rng, dims, scale, reach, cuts=(), held_as=jnp.bfloat16):
    values = jax.random.normal(rng, dims, jnp.float32) * scale
    if len(cuts) > 0:
        values = block_scale(rng, dims, cuts, -0.22, 0.18) * values
    return jnp.clip(values, min=-reach, max=reach).astype(held_as)


def setup_inputs(seed: int = 0, part: int = 0) -> dict:
    keys = jax.random.split(jax.random.key(seed), 21)
    part_splits = jax.random.split(jax.random.fold_in(keys[20], part), 21)
    span_query = noise(part_splits[0], (SPAN_TOKENS, HK, DK), 1.0, 6.0, ((0, 16), (1, 4)))
    span_key = draw_span_key(jax.random.fold_in(jax.random.fold_in(keys[20], part), 71), part)
    span_value = noise(part_splits[2], (SPAN_TOKENS, VALUE_HEADS, DV), 1.0, 6.0, ((0, 16), (1, 4)))
    span_beta_logit = jnp.clip(-5.0 + 3.0 * jax.random.uniform(part_splits[3], (SPAN_TOKENS, VALUE_HEADS), jnp.float32) ** block_scale(part_splits[3], (SPAN_TOKENS, VALUE_HEADS), ((0, 16), (1, 4)), -0.2, 0.2), -5.0, -2.0)
    span_logdecay = draw_span_logdecay(jax.random.fold_in(jax.random.fold_in(keys[20], part), 71), part)
    span_gate = noise(part_splits[5], (SPAN_TOKENS, VALUE_HEADS, DV), 1.0, 6.0, ((0, 16), (1, 4)))
    norm_gain = jnp.clip(1.0 + 0.18 * jax.random.normal(keys[6], (DV,), jnp.float32), 0.1, 1.9)
    prior_state = noise(part_splits[7], (VALUE_HEADS, DK, DV), 0.2, 1.25, ((0, 4),), jnp.float32)
    step_query = noise(part_splits[8], (SAMPLES, STEPS, HK, DK), 1.0, 6.0, ((0, 16), (2, 4)))
    step_key = noise(part_splits[9], (SAMPLES, STEPS, HK, DK), 1.0, 6.0, ((0, 16), (2, 4)))
    step_value = noise(part_splits[10], (SAMPLES, STEPS, VALUE_HEADS, DV), 1.0, 6.0, ((0, 16), (2, 4)))
    step_beta_logit = jnp.clip(-2.0 + 3.0 * jax.random.uniform(part_splits[11], (SAMPLES, STEPS, VALUE_HEADS), jnp.float32) ** block_scale(part_splits[11], (SAMPLES, STEPS, VALUE_HEADS), ((0, 16), (2, 4)), -0.2, 0.2), -2.0, 1.0)
    step_logdecay = jnp.clip(-0.7 + 0.68 * jax.random.uniform(part_splits[12], (SAMPLES, STEPS, VALUE_HEADS), jnp.float32) ** block_scale(part_splits[12], (SAMPLES, STEPS, VALUE_HEADS), ((0, 16), (2, 4)), -0.2, 0.2), -0.7, -0.02)
    step_gate = noise(part_splits[13], (SAMPLES, STEPS, VALUE_HEADS, DV), 1.0, 6.0, ((0, 16), (2, 4)))
    cache_key = draw_cache_key(jax.random.fold_in(jax.random.fold_in(keys[20], part), 71), part)
    cache_value = noise(part_splits[15], (CTX, KVH, HD), 1.0, 6.0, ((0, 16),))
    att_query = draw_att_query(jax.random.fold_in(jax.random.fold_in(keys[20], part), 71), part)
    att_key = draw_att_key(jax.random.fold_in(jax.random.fold_in(keys[20], part), 71), part)
    att_value = noise(part_splits[18], (SAMPLES, STEPS, KVH, HD), 1.0, 6.0, ((0, 16),))
    att_gate = noise(part_splits[19], (SAMPLES, STEPS, QH, HD), 1.0, 6.0, ((0, 16), (2, 4)))
    return {"span_query": span_query, "span_key": span_key, "span_value": span_value, "span_beta_logit": span_beta_logit, "span_logdecay": span_logdecay, "span_gate": span_gate, "norm_gain": norm_gain, "prior_state": prior_state, "step_query": step_query, "step_key": step_key, "step_value": step_value, "step_beta_logit": step_beta_logit, "step_logdecay": step_logdecay, "step_gate": step_gate, "cache_key": cache_key, "cache_value": cache_value, "att_query": att_query, "att_key": att_key, "att_value": att_value, "att_gate": att_gate}


peak_value = lax.Precision.HIGHEST

def unit_rows(values):
    values = values.astype(jnp.float32)
    return values / jnp.sqrt(lax.optimization_barrier(jnp.sum(values * values, axis=-1, keepdims=True)) + 1e-06)

def gated_norm(layer_output, gating, norm_gain):
    scaling = 1.0 / jnp.sqrt(lax.optimization_barrier(jnp.mean(layer_output * layer_output, axis=-1, keepdims=True)) + 1e-06)
    gating = gating.astype(jnp.float32)
    return layer_output * scaling * norm_gain * (gating * jax.nn.sigmoid(gating))

def delta_step(recurrent_state, query_vectors, key_matrix_rows, values, write_rate, retention):
    recalled_values = jnp.einsum('...ow,...owy->...oy', key_matrix_rows, recurrent_state, precision=peak_value)
    written = (write_rate[..., None] * key_matrix_rows)[..., :, None]
    erased = recurrent_state - written * recalled_values[..., None, :]
    recurrent_state = retention[..., None, None] * erased + written * values[..., None, :]
    layer_output = jnp.einsum('...ow,...owy->...oy', query_vectors, recurrent_state, precision=peak_value)
    return (recurrent_state, layer_output)

def attend_sample(query_vectors, own_keys, own_values, gating, cache_keys, cache_values):
    head_group = QH // KVH
    scaling = HD ** (-0.5)
    grouped = query_vectors.astype(jnp.float32).reshape(STEPS, KVH, head_group, HD)
    cache_scores = jnp.einsum('jgrk,cgk->jgrc', grouped, cache_keys) * scaling
    own_scores = jnp.einsum('jgrk,igk->jgri', grouped, own_keys.astype(jnp.float32)) * scaling
    causal = lax.broadcasted_iota(jnp.int32, (STEPS, STEPS), 0) >= lax.broadcasted_iota(jnp.int32, (STEPS, STEPS), 1)
    own_scores = jnp.where(causal[:, None, None, :], own_scores, -jnp.inf)
    row_max = jnp.maximum(lax.optimization_barrier(jnp.max(cache_scores, axis=3)), lax.optimization_barrier(jnp.max(own_scores, axis=3)))[..., None]
    cache_weights = lax.optimization_barrier(jnp.exp(cache_scores - row_max).astype(jnp.bfloat16)).astype(jnp.float32)
    own_weights = lax.optimization_barrier(jnp.exp(own_scores - row_max).astype(jnp.bfloat16)).astype(jnp.float32)
    numerator = jnp.einsum('jgrc,cgk->jgrk', cache_weights, cache_values)
    numerator = numerator + jnp.einsum('jgri,igk->jgrk', own_weights, own_values.astype(jnp.float32))
    denominator = lax.optimization_barrier(jnp.sum(cache_weights, axis=3)) + lax.optimization_barrier(jnp.sum(own_weights, axis=3))
    gate_values = jax.nn.sigmoid(gating.astype(jnp.float32).reshape(STEPS, KVH, head_group, HD))
    layer_output = numerator / denominator[..., None] * gate_values
    return layer_output.reshape(STEPS, QH * HD).astype(jnp.bfloat16)

def reference(span_query, span_key, span_value, span_beta_logit, span_logdecay, span_gate, norm_gain, prior_state, step_query, step_key, step_value, step_beta_logit, step_logdecay, step_gate, cache_key, cache_value, att_query, att_key, att_value, att_gate):
    ratio_heads = VALUE_HEADS // HK
    query_vectors = jnp.repeat(unit_rows(span_query) * DK ** (-0.5), ratio_heads, axis=1)
    key_matrix_rows = jnp.repeat(unit_rows(span_key), ratio_heads, axis=1)
    values = span_value.astype(jnp.float32)
    write_rate = jax.nn.sigmoid(span_beta_logit)
    retention = jnp.exp(span_logdecay)

    def advance(recurrent_state, inputs):
        return delta_step(recurrent_state, inputs[0], inputs[1], inputs[2], inputs[3], inputs[4])
    prompt_state, span_kernel_body = lax.scan(advance, prior_state, (query_vectors, key_matrix_rows, values, write_rate, retention))
    span_out = gated_norm(span_kernel_body, span_gate, norm_gain).astype(jnp.bfloat16).reshape(SPAN_TOKENS, VALUE_HEADS * DV)
    step_queries = jnp.repeat(unit_rows(step_query) * DK ** (-0.5), ratio_heads, axis=2)
    step_keys = jnp.repeat(unit_rows(step_key), ratio_heads, axis=2)
    step_values = step_value.astype(jnp.float32)
    step_rate = jax.nn.sigmoid(step_beta_logit)
    step_retention = jnp.exp(step_logdecay)
    recurrent_state = jnp.broadcast_to(prompt_state, (SAMPLES, VALUE_HEADS, DK, DV))
    outputs = []
    for step_index in range(STEPS):
        recurrent_state, layer_output = delta_step(recurrent_state, step_queries[:, step_index], step_keys[:, step_index], step_values[:, step_index], step_rate[:, step_index], step_retention[:, step_index])
        outputs.append(layer_output)
    step_core = jnp.stack(outputs, axis=1)
    step_out = gated_norm(step_core, step_gate, norm_gain).astype(jnp.bfloat16).reshape(SAMPLES, STEPS, VALUE_HEADS * DV)
    cache_keys = cache_key.astype(jnp.float32)
    cache_values = cache_value.astype(jnp.float32)

    def one_sample(pieces):
        return attend_sample(pieces[0], pieces[1], pieces[2], pieces[3], cache_keys, cache_values)
    att_out = lax.map(one_sample, (att_query, att_key, att_value, att_gate))
    return (span_out, step_out, recurrent_state, att_out)
```

```python
import functools

import jax
import jax.numpy as jnp
from jax import lax
from jax.experimental import pallas as pl
from jax.experimental.pallas import tpu as pltpu
from jax.sharding import PartitionSpec as P

F32 = jnp.float32
BF16 = jnp.bfloat16
MESH = pl.DeviceIdType.MESH
EPS = 1e-6
C = 128
D = 128
HEADS = 8
KHEADS = 4
TOK = 512
NCH = TOK // C
HALF = 8
WIDE = 16
NEG = -1e30


def dot(a, b):
    return lax.dot_general(a, b, (((1,), (0,)), ((), ())), preferred_element_type=F32)


def dot_nt(a, b):
    return lax.dot_general(a, b, (((1,), (1,)), ((), ())), preferred_element_type=F32)


def dot_tn(a, b):
    return lax.dot_general(a, b, (((0,), (0,)), ((), ())), preferred_element_type=F32)


def split(x):
    hi = x.astype(BF16)
    return hi, (x - hi.astype(F32)).astype(BF16)


def sigmoid(x):
    return 1.0 / (1.0 + jnp.exp(-x))


def span_kernel(q_ref, k_ref, v_ref, s_ref, wire_ref, o_ref, g_ref, qf, kf, vf):
    qf[...] = q_ref[...].astype(F32)
    kf[...] = k_ref[...].astype(F32)
    vf[...] = v_ref[...].astype(F32)
    row = lax.broadcasted_iota(jnp.int32, (C, C), 0)
    col = lax.broadcasted_iota(jnp.int32, (C, C), 1)
    upper = (row <= col).astype(F32)

    def head(kh, _):
        rp = [None, None]
        acc = [None, None]
        for c in range(NCH):
            k32 = kf[pl.ds(c * C * KHEADS + kh, C, stride=KHEADS), :]
            q32 = qf[pl.ds(c * C * KHEADS + kh, C, stride=KHEADS), :]
            k16 = k32.astype(BF16)
            q16 = q32.astype(BF16)
            kt16 = k32.T.astype(BF16)
            kk = dot(k16, kt16)
            qk = dot(q16, kt16)
            eye = jnp.where(row == col, kk, 0.0)
            rk_row = lax.rsqrt(jnp.sum(eye, axis=0, keepdims=True) + EPS)
            rk = lax.rsqrt(jnp.sum(k32 * k32, axis=1, keepdims=True) + EPS)
            rq = lax.rsqrt(jnp.sum(q32 * q32, axis=1, keepdims=True) + EPS) * (D**-0.5)
            kkn = kk * rk * rk_row
            qkn = qk * rq * rk_row
            rows = s_ref[kh, :, c * C : (c + 1) * C]
            g_rows = lax.dot_general(
                rows, upper, (((1,), (0,)), ((), ())),
                precision=lax.Precision.HIGHEST, preferred_element_type=F32,
            )
            pick = lax.broadcasted_iota(jnp.int32, (8, C), 0) < 2
            mixed = jnp.where(pick, g_rows, sigmoid(rows))
            cols = mixed.T
            for e in range(2):
                g_row = g_rows[e : e + 1, :]
                g = cols[:, e : e + 1]
                b = cols[:, 2 + e : 3 + e]
                ratio = jnp.exp(jnp.where(row >= col, g - g_row, NEG))
                low = jnp.where(row > col, ratio * kkn * b, 0.0)
                sc = ratio * qkn
                near = jnp.where((row >> 1) == (col >> 1), low, 0.0)
                inv = -near
                for lg in range(1, 7):
                    off = jnp.where(
                        ((row >> (lg + 1)) == (col >> (lg + 1))) & ((row >> lg) != (col >> lg)),
                        low, 0.0,
                    )
                    inv16 = inv.astype(BF16)
                    y = off + dot(inv16, off.astype(BF16))
                    inv = inv - (y + dot(y.astype(BF16), inv16))
                eg = jnp.exp(g)
                g_end = g[C - 1 : C, :]
                e_end = jnp.exp(g_end)
                v32 = vf[pl.ds(c * C * HEADS + 2 * kh + e, C, stride=HEADS), :]
                rhs = jnp.concatenate([b * v32, (b * eg * rk) * k32], axis=1)
                x = rhs + dot(inv.astype(BF16), rhs.astype(BF16))
                u0, w = x[:, :D], x[:, D:]
                if c == 0:
                    uw = jnp.concatenate([u0, -w], axis=1)
                    base = None
                else:
                    rp16 = rp[e].astype(BF16)
                    wrp = dot(w.astype(BF16), rp16)
                    uw = jnp.concatenate(
                        [u0 - wrp[:, :D], -(acc[e] * w + wrp[:, D:])], axis=1
                    )
                    base = (eg * rq) * dot(q16, rp16)
                sch, scl = split(sc)
                uh, ul = split(uw)
                og = dot(sch, uh) + dot(scl, uh) + dot(sch, ul)
                if base is not None:
                    og = og + base
                direct = (eg * rq) if c == 0 else (eg * rq) * acc[e]
                hd = 2 * kh + e
                o_ref[hd, c * C : (c + 1) * C, :] = og[:, :D]
                gh, gl = split(og[:, D:] + direct * q32)
                g_ref[hd, c * C : (c + 1) * C, :D] = gh
                g_ref[hd, c * C : (c + 1) * C, D:] = gl
                sh, sl = split((jnp.exp(g_end - g) * rk) * uw)
                add = dot(kt16, sh) + dot(kt16, sl)
                if c == 0:
                    rp[e] = add
                    acc[e] = e_end
                else:
                    rp[e] = e_end * rp[e] + add
                    acc[e] = e_end * acc[e]
        for e in range(2):
            hd = 2 * kh + e
            bh, bl = split(rp[e][:, :D])
            wire_ref[hd, 0:C, 0:D] = rp[e][:, D:].astype(BF16)
            wire_ref[hd, 0:C, D : 2 * D] = bh
            wire_ref[hd, 0:C, 2 * D : 3 * D] = bl
            a = jnp.broadcast_to(acc[e], (16, 3 * D))
            a0 = a.astype(BF16).astype(F32)
            a1 = (a - a0).astype(BF16).astype(F32)
            a2 = a - a0 - a1
            lane = lax.broadcasted_iota(jnp.int32, (16, 3 * D), 1)
            wire_ref[hd, C : C + 16, :] = jnp.where(
                lane < D, a0, jnp.where(lane < 2 * D, a1, a2)
            ).astype(BF16)
        return 0

    lax.fori_loop(0, KHEADS, head, 0)


def span_local(q, k, v, scal):
    vm = pl.BlockSpec(memory_space=pltpu.VMEM)
    return pl.pallas_call(
        span_kernel,
        out_shape=(
            jax.ShapeDtypeStruct((HEADS, C + 16, 3 * D), BF16),
            jax.ShapeDtypeStruct((HEADS, TOK, D), F32),
            jax.ShapeDtypeStruct((HEADS, TOK, 2 * D), BF16),
        ),
        in_specs=[vm] * 4,
        out_specs=(vm, vm, vm),
        scratch_shapes=[
            pltpu.VMEM((TOK * KHEADS, D), F32),
            pltpu.VMEM((TOK * KHEADS, D), F32),
            pltpu.VMEM((TOK * HEADS, D), F32),
        ],
        compiler_params=pltpu.CompilerParams(vmem_limit_bytes=40 * 2**20),
        cost_estimate=pl.CostEstimate(flops=8 * 10**9, bytes_accessed=8 * 2**20, transcendentals=0),
        name="span_local",
    )(q, k, v, scal)


def attention_kernel(q_ref, k_ref, v_ref, m_ref, sc_ref):
    sc_ref[...] = dot_nt(q_ref[...], k_ref[...]) * (256**-0.5)
    scores = sc_ref[...]
    top = jnp.max(scores, axis=1, keepdims=True)
    w = jnp.exp(scores - top).astype(BF16)
    total = jnp.sum(w.astype(F32), axis=1, keepdims=True)
    out = dot(w, v_ref[...]) / total
    level = top + jnp.log(total)
    l0 = level.astype(BF16).astype(F32)
    l1 = (level - l0).astype(BF16).astype(F32)
    l2 = level - l0 - l1
    lane = lax.broadcasted_iota(jnp.int32, (256, 256), 1)
    packed = jnp.where(lane < 64, l0, jnp.where(lane < 128, l1, l2)).astype(BF16)
    out = out.astype(BF16)
    for s in range(WIDE):
        m_ref[s, 0:16, :] = out[s * 16 : (s + 1) * 16, :]
        m_ref[s, 16:32, :] = packed[s * 16 : (s + 1) * 16, :]


def attention_local(q, k, v):
    vm = pl.BlockSpec(memory_space=pltpu.VMEM)
    return pl.pallas_call(
        attention_kernel,
        out_shape=jax.ShapeDtypeStruct((WIDE, 32, 256), BF16),
        in_specs=[vm] * 3,
        out_specs=vm,
        scratch_shapes=[pltpu.VMEM((256, 2048), F32)],
        compiler_params=pltpu.CompilerParams(vmem_limit_bytes=32 * 2**20),
        cost_estimate=pl.CostEstimate(flops=6 * 10**8, bytes_accessed=3 * 2**20, transcendentals=2**19),
        name="attention_local",
    )(q, k, v)


def exchange_kernel(
    wire_ref, prior_ref, att_ref, sin_ref, fin_ref, parts_ref,
    maps, ent, mul, mid, finp, last,
    att_s, att_r, map_s, map_r, sin_s, sin_r, fin_s, fin_r, z_s, z_r,
):
    w = lax.axis_index("wide")
    zh = w // HALF
    j = w % HALF

    barrier = pltpu.get_barrier_semaphore()
    for d in range(1, WIDE):
        pl.semaphore_signal(
            barrier, inc=1, device_id={"wide": (w + d) % WIDE}, device_id_type=MESH
        )
    pl.semaphore_wait(barrier, WIDE - 1)

    def peer(d):
        return zh * HALF + (j + d) % HALF

    map_copies = []
    for d in range(1, HALF):
        to = (j + d) % HALF
        copy = pltpu.make_async_remote_copy(
            src_ref=wire_ref.at[to], dst_ref=maps.at[j],
            send_sem=map_s.at[d], recv_sem=map_r.at[d],
            device_id={"wide": peer(d)}, device_id_type=MESH,
        )
        copy.start()
        map_copies.append(copy)
    att_copies = []
    for d in range(1, WIDE):
        to = (w + d) % WIDE
        copy = pltpu.make_async_remote_copy(
            src_ref=att_ref.at[to], dst_ref=parts_ref.at[w],
            send_sem=att_s.at[d], recv_sem=att_r.at[d],
            device_id={"wide": to}, device_id_type=MESH,
        )
        copy.start()
        att_copies.append(copy)
    maps[j] = wire_ref[j]
    parts_ref[w] = att_ref[w]
    for copy in map_copies:
        copy.wait_recv()

    first = jnp.where(zh == 0, 1.0, 0.0)
    ent[0] = jnp.concatenate([prior_ref[j] * first, jnp.zeros((D, D), F32)], axis=1)
    mul[0] = jnp.ones((8, D), F32)

    def link(i, _):
        m16 = maps[i, 0:C, 0:D]
        add = maps[i, 0:C, D : 2 * D].astype(F32) + maps[i, 0:C, 2 * D : 3 * D].astype(F32)
        ar = maps[i, C : C + 16, :].astype(F32)
        a = (ar[0:8, 0:D] + ar[0:8, D : 2 * D]) + ar[0:8, 2 * D : 3 * D]
        x = ent[i]
        xh, xl = split(x)
        mx = dot(m16, xh) + dot(m16, xl)
        acc = mul[i]
        a1 = a[0:1, :]
        r = a1 * x[:, :D] + mx[:, :D] + add
        p = a1 * x[:, D:] + mx[:, D:] + acc[0:1, :] * m16.astype(F32)
        ent[i + 1] = jnp.concatenate([r, p], axis=1)
        mul[i + 1] = a * acc
        return 0

    lax.fori_loop(0, HALF, link, 0)

    @pl.when(zh == 0)
    def _():
        last[...] = ent[HALF, :, 0:D]
        copy = pltpu.make_async_remote_copy(
            src_ref=last, dst_ref=mid, send_sem=z_s.at[0], recv_sem=z_r.at[0],
            device_id={"wide": j + HALF}, device_id_type=MESH,
        )
        copy.start()
        copy.wait_send()

    @pl.when(zh == 1)
    def _():
        pltpu.make_async_remote_copy(
            src_ref=last, dst_ref=mid, send_sem=z_s.at[0], recv_sem=z_r.at[0],
            device_id={"wide": j}, device_id_type=MESH,
        ).wait_recv()
        s = mid[...]
        sh, sl = split(s)
        both = jnp.concatenate([sh, sl], axis=1)

        def enter(i, _):
            x = ent[i]
            ph, pl_ = split(x[:, D:])
            y = dot(ph, both)
            ent[i, :, 0:D] = (
                x[:, :D] + mul[i, 0:1, :] * s + y[:, :D] + y[:, D:] + dot(pl_, sh)
            )
            return 0

        lax.fori_loop(0, HALF + 1, enter, 0)
        finp[...] = ent[HALF, :, 0:D]

    sin_copies = []
    stage = maps_stage = None
    for d in range(1, HALF):
        to = (j + d) % HALF
        copy = pltpu.make_async_remote_copy(
            src_ref=ent.at[to, :, pl.ds(0, D)], dst_ref=sin_ref.at[j],
            send_sem=sin_s.at[d], recv_sem=sin_r.at[d],
            device_id={"wide": peer(d)}, device_id_type=MESH,
        )
        copy.start()
        sin_copies.append(copy)
    sin_ref[j] = ent[j, :, 0:D]

    @pl.when(zh == 1)
    def _():
        copy = pltpu.make_async_remote_copy(
            src_ref=finp, dst_ref=finp, send_sem=z_s.at[1], recv_sem=z_r.at[1],
            device_id={"wide": j}, device_id_type=MESH,
        )
        copy.start()
        copy.wait_send()

    @pl.when(zh == 0)
    def _():
        pltpu.make_async_remote_copy(
            src_ref=finp, dst_ref=finp, send_sem=z_s.at[1], recv_sem=z_r.at[1],
            device_id={"wide": j + HALF}, device_id_type=MESH,
        ).wait_recv()

    fin_copies = []
    for d in range(1, HALF):
        copy = pltpu.make_async_remote_copy(
            src_ref=finp, dst_ref=fin_ref.at[j],
            send_sem=fin_s.at[d], recv_sem=fin_r.at[d],
            device_id={"wide": peer(d)}, device_id_type=MESH,
        )
        copy.start()
        fin_copies.append(copy)
    fin_ref[j] = finp[...]
    for copy in map_copies:
        copy.wait_send()
    for copy in att_copies + sin_copies + fin_copies:
        copy.wait()


def exchange(wire, prior, att):
    vm = pl.BlockSpec(memory_space=pltpu.VMEM)
    sem = pltpu.SemaphoreType.DMA
    return pl.pallas_call(
        exchange_kernel,
        out_shape=(
            jax.ShapeDtypeStruct((HEADS, D, D), F32),
            jax.ShapeDtypeStruct((HEADS, D, D), F32),
            jax.ShapeDtypeStruct((WIDE, 32, 256), BF16),
        ),
        in_specs=[vm] * 3,
        out_specs=(vm, vm, vm),
        scratch_shapes=[
            pltpu.VMEM((HALF, C + 16, 3 * D), BF16),
            pltpu.VMEM((HALF + 1, D, 2 * D), F32),
            pltpu.VMEM((HALF + 1, 8, D), F32),
            pltpu.VMEM((D, D), F32),
            pltpu.VMEM((D, D), F32),
            pltpu.VMEM((D, D), F32),
            sem((WIDE,)), sem((WIDE,)),
            sem((HALF,)), sem((HALF,)),
            sem((HALF,)), sem((HALF,)),
            sem((HALF,)), sem((HALF,)),
            sem((2,)), sem((2,)),
        ],
        compiler_params=pltpu.CompilerParams(
            collective_id=0, has_side_effects=True, vmem_limit_bytes=32 * 2**20
        ),
        name="exchange",
    )(wire, prior, att)


def output_kernel(
    o_ref, g_ref, sin_ref, fin_ref, gate_ref, gain_ref,
    kq_ref, sv_ref, sb_ref, sd_ref, sg_ref,
    parts_ref, aq_ref, ak_ref, av_ref, ag_ref,
    out_ref, step_ref, state_ref, att_ref,
    gatef, res, uscr,
):
    gain = gain_ref[...]
    gatef[...] = gate_ref[...].astype(F32)

    def head(h, _):
        s = sin_ref[h]
        sh, sl = split(s)
        both = jnp.concatenate([sh, sl], axis=1)
        both = jnp.concatenate([both, both], axis=0)
        y = dot(g_ref[h], both)
        o = o_ref[h] + (y[:, :D] + y[:, D:])
        scale = lax.rsqrt(jnp.mean(o * o, axis=1, keepdims=True) + EPS)
        z = gatef[pl.ds(h, TOK, stride=HEADS), :]
        r = (o * scale * gain * (z * sigmoid(z))).astype(BF16)
        out_ref[:, pl.ds(pl.multiple_of(h * D, D), D)] = r
        return 0

    lax.fori_loop(0, HEADS, head, 0)

    def recall(h, _):
        sh, sl = split(fin_ref[h])
        both = jnp.concatenate([sh, sl], axis=1)
        y = dot(kq_ref[h].astype(BF16), both)
        res[pl.ds(pl.multiple_of(h * 8, 8), 8), :] = y[:, :D] + y[:, D:]
        return 0

    lax.fori_loop(0, HEADS, recall, 0)
    kraw = [kq_ref[:, i, :] for i in range(4)]
    qraw = [kq_ref[:, 4 + i, :] for i in range(4)]
    rk = [lax.rsqrt(jnp.sum(x * x, axis=1, keepdims=True) + EPS) for x in kraw]
    rq = [lax.rsqrt(jnp.sum(x * x, axis=1, keepdims=True) + EPS) * (D**-0.5) for x in qraw]
    kn = [x * r for x, r in zip(kraw, rk)]
    qn = [x * r for x, r in zip(qraw, rq)]
    beta = sigmoid(sb_ref[...])
    ld = sd_ref[...]
    cum = [ld[:, 0:1]]
    for i in range(1, 4):
        cum.append(cum[-1] + ld[:, i : i + 1])
    us = []
    for i in range(4):
        ks = res[pl.ds(i, HEADS, stride=8), :] * (rk[i] * jnp.exp(cum[i]))
        u = sv_ref[i].astype(F32) - ks
        for p in range(i):
            kk = jnp.sum(kn[i] * kn[p], axis=1, keepdims=True)
            u = u - (jnp.exp(cum[i] - cum[p]) * kk) * us[p]
        u = beta[:, i : i + 1] * u
        us.append(u)
        o = res[pl.ds(4 + i, HEADS, stride=8), :] * (rq[i] * jnp.exp(cum[i]))
        for p in range(i + 1):
            qk = jnp.sum(qn[i] * kn[p], axis=1, keepdims=True)
            o = o + (jnp.exp(cum[i] - cum[p]) * qk) * us[p]
        scale = lax.rsqrt(jnp.mean(o * o, axis=1, keepdims=True) + EPS)
        z = sg_ref[i].astype(F32)
        step_ref[i] = (o * scale * gain * (z * sigmoid(z))).astype(BF16)
    for i in range(4):
        uscr[pl.ds(i, HEADS, stride=8), :] = us[i] * (jnp.exp(cum[3] - cum[i]) * rk[i])
        uscr[pl.ds(4 + i, HEADS, stride=8), :] = jnp.zeros((HEADS, D), F32)
    decay = jnp.broadcast_to(jnp.exp(cum[3]), (HEADS, D))
    for h in range(HEADS):
        uh, ul = split(uscr[h * 8 : (h + 1) * 8, :])
        both = jnp.concatenate([uh, ul], axis=1)
        y = dot_tn(kq_ref[h].astype(BF16), both)
        state_ref[h] = decay[h : h + 1, :] * fin_ref[h] + (y[:, :D] + y[:, D:])

    tp = lax.axis_index("tp")
    group = tp // 2
    aq = aq_ref[...]
    own = dot_nt(aq, ak_ref[...]) * (256**-0.5)
    r = lax.broadcasted_iota(jnp.int32, (16, 8), 0) // 4
    cc = lax.broadcasted_iota(jnp.int32, (16, 8), 1)
    own = jnp.where((cc % 2 == group) & (cc // 2 <= r), own, NEG)
    top = jnp.max(own, axis=1, keepdims=True)
    levels = []
    for s in range(WIDE):
        packed = parts_ref[s, 16:32, :].astype(F32)
        lv = (packed[:, 0:1] + packed[:, 64:65]) + packed[:, 128:129]
        levels.append(lv)
        top = jnp.maximum(top, lv)
    pw = jnp.exp(own - top).astype(BF16)
    den = jnp.sum(pw.astype(F32), axis=1, keepdims=True)
    num = dot(pw, av_ref[...])
    for s in range(WIDE):
        wt = jnp.exp(levels[s] - top)
        den = den + wt
        num = num + wt * parts_ref[s, 0:16, :].astype(F32)
    att_ref[...] = (num / den * sigmoid(ag_ref[...].astype(F32))).astype(BF16)


def outputs(*args):
    vm = pl.BlockSpec(memory_space=pltpu.VMEM)
    return pl.pallas_call(
        output_kernel,
        out_shape=(
            jax.ShapeDtypeStruct((TOK, HEADS * D), BF16),
            jax.ShapeDtypeStruct((4, HEADS, D), BF16),
            jax.ShapeDtypeStruct((HEADS, D, D), F32),
            jax.ShapeDtypeStruct((16, 256), BF16),
        ),
        in_specs=[vm] * 16,
        out_specs=(vm,) * 4,
        scratch_shapes=[
            pltpu.VMEM((TOK * HEADS, D), F32),
            pltpu.VMEM((64, D), F32),
            pltpu.VMEM((64, D), F32),
        ],
        compiler_params=pltpu.CompilerParams(vmem_limit_bytes=40 * 2**20),
        name="outputs",
    )(*args)


def shards(
    span_query, span_key, span_value, span_beta_logit, span_logdecay, span_gate,
    norm_gain, prior_state,
    step_query, step_key, step_value, step_beta_logit, step_logdecay, step_gate,
    cache_key, cache_value, att_query, att_key, att_value, att_gate,
):
    q = span_query.reshape(TOK * KHEADS, D)
    k = span_key.reshape(TOK * KHEADS, D)
    v = span_value.reshape(TOK * HEADS, D)
    gate = span_gate.reshape(TOK * HEADS, D)
    ldt = span_logdecay.T.reshape(KHEADS, 2, TOK)
    blt = span_beta_logit.T.reshape(KHEADS, 2, TOK)
    scal = jnp.concatenate([ldt, blt, jnp.zeros((KHEADS, 4, TOK), F32)], axis=1)
    every_query = lax.all_gather(att_query, "wide", axis=0, tiled=True).reshape(256, 256)
    group = lax.axis_index("tp") // 2
    keys = lax.dynamic_index_in_dim(cache_key, group, axis=1, keepdims=False)
    values = lax.dynamic_index_in_dim(cache_value, group, axis=1, keepdims=False)
    wire, o0, g = span_local(q, k, v, scal)
    att = attention_local(every_query, keys, values)
    sin, fin, parts = exchange(wire, prior_state, att)
    kq = jnp.repeat(
        jnp.concatenate([step_key[0], step_query[0]], axis=0).transpose(1, 0, 2), 2, axis=0
    ).astype(F32)
    out, step, state, att_out = outputs(
        o0, g, sin, fin, gate, norm_gain.reshape(1, D),
        kq, step_value[0], step_beta_logit[0].T, step_logdecay[0].T, step_gate[0],
        parts, att_query.reshape(16, 256), att_key.reshape(8, 256), att_value.reshape(8, 256),
        att_gate.reshape(16, 256),
    )
    return (
        out, step.reshape(1, 4, HEADS * D), state[None], att_out.reshape(1, 4, 1024)
    )


def solution(mesh):
    tok = P(("prompt", "wide"), "tp", None)
    tok2 = P(("prompt", "wide"), "tp")
    stp = P(("prompt", "wide"), None, "tp", None)
    stp2 = P(("prompt", "wide"), None, "tp")
    in_specs = (
        tok, tok, tok, tok2, tok2, tok, P(), P(("prompt", "tp"), None, None),
        stp, stp, stp, stp2, stp2, stp,
        P(("prompt", "wide"), None, None), P(("prompt", "wide"), None, None),
        stp, P(("prompt", "wide"), None, None, None), P(("prompt", "wide"), None, None, None), stp,
    )
    out_specs = (
        P(("prompt", "wide"), "tp"),
        stp2,
        P(("prompt", "wide"), "tp", None, None),
        stp2,
    )
    return jax.shard_map(shards, mesh=mesh, in_specs=in_specs, out_specs=out_specs, check_vma=False)
```

```python
import jax
import jax.numpy as jnp
from jax import lax
from jax.experimental import pallas as pl
from jax.experimental.pallas import tpu as pltpu
from jax.sharding import PartitionSpec as P

F32 = jnp.float32
BF16 = jnp.bfloat16
MESH = pl.DeviceIdType.MESH
EPS = 1e-6
C = 128
D = 128
HEADS = 8
KHEADS = 4
TOK = 512
NCH = TOK // C
HALF = 8
WIDE = 16
NEG = -1e30


def dot(a, b):
    return lax.dot_general(a, b, (((1,), (0,)), ((), ())), preferred_element_type=F32)


def dot_nt(a, b):
    return lax.dot_general(a, b, (((1,), (1,)), ((), ())), preferred_element_type=F32)


def dot_tn(a, b):
    return lax.dot_general(a, b, (((0,), (0,)), ((), ())), preferred_element_type=F32)


def split(x):
    hi = x.astype(BF16)
    return hi, (x - hi.astype(F32)).astype(BF16)


def sigmoid(x):
    return 1.0 / (1.0 + jnp.exp(-x))


def kernel(
    q_hbm, k_hbm, v_hbm, bl_ref, ld_ref, gate_hbm, gain_ref, prior_hbm,
    sq_ref, sk_ref, sv_ref, sb_ref, sd_ref, sg_ref,
    ck_hbm, cv_hbm, aq_ref, ak_ref, av_ref, ag_ref,
    out_ref, step_ref, state_ref, att_ref,
    qv, kv, vv, gv, ckv, cvv, prior,
    qf, kf, vf, cf, kc, vc, scores, scal,
    wire, maps, o0, gq, ent, mul, mid, fin_z,
    sin16, sin, finp, fin, own_q, all_q, msg, parts,
    kqs, res, uscr, sscr, a0s, a1s, own_k,
    load, q_s, q_r, att_s, att_r, map_s, map_r, sin_s, sin_r, fin_s, fin_r, z_s, z_r,
):
    w = lax.axis_index("wide")
    zh = w // HALF
    j = w % HALF
    group = lax.axis_index("tp") // 2

    loads = []
    for i, (src, dst) in enumerate((
        (ck_hbm, ckv), (cv_hbm, cvv), (q_hbm, qv), (k_hbm, kv), (v_hbm, vv), (gate_hbm, gv),
        (prior_hbm.at[j], prior),
    )):
        copy = pltpu.make_async_copy(src, dst, load.at[i])
        copy.start()
        loads.append(copy)

    barrier = pltpu.get_barrier_semaphore()
    for d in range(1, WIDE):
        pl.semaphore_signal(
            barrier, inc=1, device_id={"wide": (w + d) % WIDE}, device_id_type=MESH
        )
    for i in range(4):
        a0s[4 * i : 4 * i + 4, :] = aq_ref[0, i].astype(F32)
    own_q[...] = a0s[...].astype(BF16)
    pl.semaphore_wait(barrier, WIDE - 1)

    def remote(src, dst, ss, rs, to):
        return pltpu.make_async_remote_copy(
            src_ref=src, dst_ref=dst, send_sem=ss, recv_sem=rs,
            device_id={"wide": to}, device_id_type=MESH,
        )

    def map_copy(to, slot, device):
        return remote(wire.at[to], maps.at[slot], map_s.at[to], map_r.at[slot], device)

    q_copies = []
    for d in range(1, WIDE):
        copy = remote(own_q, all_q.at[w], q_s.at[d], q_r.at[d], (w + d) % WIDE)
        copy.start()
        q_copies.append(copy)
    all_q[w] = own_q[...]

    upper = (
        lax.broadcasted_iota(jnp.int32, (C, C), 0) <= lax.broadcasted_iota(jnp.int32, (C, C), 1)
    ).astype(F32)
    scal[...] = jnp.zeros_like(scal)
    for c in range(NCH):
        part = slice(c * C, (c + 1) * C)
        g8 = lax.dot_general(
            ld_ref[:, part], upper, (((1,), (0,)), ((), ())),
            precision=lax.Precision.HIGHEST, preferred_element_type=F32,
        )
        b8 = sigmoid(bl_ref[:, part])
        for kh in range(KHEADS):
            scal[kh, 0:2, part] = g8[2 * kh : 2 * kh + 2]
            scal[kh, 2:4, part] = b8[2 * kh : 2 * kh + 2]

    for load_copy, raw, cut in ((loads[0], ckv, kc), (loads[1], cvv, vc)):
        load_copy.wait()
        cf[...] = raw[...].astype(F32)
        cut[:, 0:128] = cf[pl.ds(group, 2048, stride=4), :].astype(BF16)
        cut[:, 128:256] = cf[pl.ds(2 + group, 2048, stride=4), :].astype(BF16)
    for copy in loads[2:]:
        copy.wait()
    qf[...] = qv[...].astype(F32)
    kf[...] = kv[...].astype(F32)
    vf[...] = vv[...].astype(F32)

    for copy in q_copies:
        copy.wait()
    scores[...] = dot_nt(all_q[...].reshape(256, 256), kc[...]) * (256**-0.5)
    sc = scores[...]
    top = jnp.max(sc, axis=1, keepdims=True)
    wt = jnp.exp(sc - top).astype(BF16)
    total = jnp.sum(wt.astype(F32), axis=1, keepdims=True)
    num = (dot(wt, vc[...]) / total).astype(BF16)
    level = top + jnp.log(total)
    l0 = level.astype(BF16).astype(F32)
    l1 = (level - l0).astype(BF16).astype(F32)
    l2 = level - l0 - l1
    lane = lax.broadcasted_iota(jnp.int32, (256, 256), 1)
    packed = jnp.where(lane < 64, l0, jnp.where(lane < 128, l1, l2)).astype(BF16)
    for s in range(WIDE):
        msg[s, 0:16, :] = num[s * 16 : (s + 1) * 16, :]
        msg[s, 16:32, :] = packed[s * 16 : (s + 1) * 16, :]
    att_copies = []
    for d in range(1, WIDE):
        to = (w + d) % WIDE
        copy = remote(msg.at[to], parts.at[w], att_s.at[d], att_r.at[d], to)
        copy.start()
        att_copies.append(copy)
    parts[w] = msg[w]

    row = lax.broadcasted_iota(jnp.int32, (C, C), 0)
    col = lax.broadcasted_iota(jnp.int32, (C, C), 1)

    def head(it, _):
        kh = (j // 2 + jnp.where(it == 0, 2, 0) + jnp.where(it == 1, 1, 0)
              + jnp.where(it == 2, 3, 0)) % KHEADS
        ks, qs, kts, cells = [], [], [], []
        for c in range(NCH):
            k32 = kf[pl.ds(c * C * KHEADS + kh, C, stride=KHEADS), :]
            q32 = qf[pl.ds(c * C * KHEADS + kh, C, stride=KHEADS), :]
            k16 = k32.astype(BF16)
            q16 = q32.astype(BF16)
            kt16 = k32.T.astype(BF16)
            kq = dot(jnp.concatenate([k16, q16], axis=0), kt16)
            kk, qk = kq[:C], kq[C:]
            eye = jnp.where(row == col, kk, 0.0)
            rk_row = lax.rsqrt(jnp.sum(eye, axis=0, keepdims=True) + EPS)
            rk = lax.rsqrt(jnp.sum(k32 * k32, axis=1, keepdims=True) + EPS)
            rq = lax.rsqrt(jnp.sum(q32 * q32, axis=1, keepdims=True) + EPS) * (D**-0.5)
            kkn = kk * rk * rk_row
            qkn = qk * rq * rk_row
            g_rows = scal[kh, :, c * C : (c + 1) * C]
            cols = g_rows.T
            for e in range(2):
                g_row = g_rows[e : e + 1, :]
                g = cols[:, e : e + 1]
                b = cols[:, 2 + e : 3 + e]
                ratio = jnp.exp(jnp.where(row >= col, g - g_row, NEG))
                low = jnp.where(row > col, ratio * kkn * b, 0.0)
                eg = jnp.exp(g)
                g_end = g[C - 1 : C, :]
                v32 = vf[pl.ds(c * C * HEADS + 2 * kh + e, C, stride=HEADS), :]
                cells.append(dict(
                    low=low, sc=split(ratio * qkn), egq=eg * rq, e_end=jnp.exp(g_end),
                    out=jnp.exp(g_end - g) * rk,
                    rhs=jnp.concatenate([b * v32, (b * eg * rk) * k32], axis=1),
                ))
            qs.append((q32, q16))
            kts.append(kt16)
        invs = [-jnp.where((row >> 1) == (col >> 1), x["low"], 0.0) for x in cells]
        for lg in range(1, 7):
            here = ((row >> (lg + 1)) == (col >> (lg + 1))) & ((row >> lg) != (col >> lg))
            offs = [jnp.where(here, x["low"], 0.0) for x in cells]
            i16 = [x.astype(BF16) for x in invs]
            ys = [o + dot(i, o.astype(BF16)) for o, i in zip(offs, i16)]
            zs = [dot(y.astype(BF16), i) for y, i in zip(ys, i16)]
            invs = [v - (y + z) for v, y, z in zip(invs, ys, zs)]
        xs = [x["rhs"] + dot(i.astype(BF16), x["rhs"].astype(BF16)) for x, i in zip(cells, invs)]
        rp, acc = [None, None], [None, None]
        for c in range(NCH):
            q32, q16 = qs[c]
            two = [cells[2 * c], cells[2 * c + 1]]
            xx = [xs[2 * c], xs[2 * c + 1]]
            if c == 0:
                uws = [jnp.concatenate([x[:, :D], -x[:, D:]], axis=1) for x in xx]
            else:
                rp16 = [r.astype(BF16) for r in rp]
                wrps = [dot(x[:, D:].astype(BF16), r) for x, r in zip(xx, rp16)]
                uws = [
                    jnp.concatenate([x[:, :D] - p[:, :D], -(a * x[:, D:] + p[:, D:])], axis=1)
                    for x, p, a in zip(xx, wrps, acc)
                ]
            sp = [split(x["out"] * u) for x, u in zip(two, uws)]
            kt2 = jnp.concatenate([kts[c], kts[c]], axis=1)
            adds = [dot(kt2, jnp.concatenate([h, l], axis=0)) for h, l in sp]
            ogs = []
            for e in range(2):
                u16 = uws[e].astype(BF16)
                ogs.append(dot(
                    jnp.concatenate(two[e]["sc"], axis=1), jnp.concatenate([u16, u16], axis=0)
                ))
            if c > 0:
                ogs = [o + x["egq"] * dot(q16, r) for o, x, r in zip(ogs, two, rp16)]
            for e in range(2):
                hd = 2 * kh + e
                x = two[e]
                direct = x["egq"] if c == 0 else x["egq"] * acc[e]
                o0[hd, c * C : (c + 1) * C, :] = ogs[e][:, :D]
                gh, gl = split(ogs[e][:, D:] + direct * q32)
                gq[hd, c * C : (c + 1) * C, :D] = gh
                gq[hd, c * C : (c + 1) * C, D:] = gl
                rp[e] = adds[e] if c == 0 else x["e_end"] * rp[e] + adds[e]
                acc[e] = x["e_end"] if c == 0 else x["e_end"] * acc[e]
        for e in range(2):
            hd = 2 * kh + e
            bh, bl = split(rp[e][:, :D])
            wire[hd, 0:C, 0:D] = rp[e][:, D:].astype(BF16)
            wire[hd, 0:C, D : 2 * D] = bh
            wire[hd, 0:C, 2 * D : 3 * D] = bl
            a = jnp.broadcast_to(acc[e], (16, 3 * D))
            a0 = a.astype(BF16).astype(F32)
            a1 = (a - a0).astype(BF16).astype(F32)
            a2 = a - a0 - a1
            lane = lax.broadcasted_iota(jnp.int32, (16, 3 * D), 1)
            wire[hd, C : C + 16, :] = jnp.where(
                lane < D, a0, jnp.where(lane < 2 * D, a1, a2)
            ).astype(BF16)

            @pl.when(hd == j)
            def _():
                maps[j] = wire[hd]

            @pl.when(hd != j)
            def _():
                map_copy(hd, j, zh * HALF + hd).start()
        return 0

    lax.fori_loop(0, KHEADS, head, 0)

    for s in range(HALF):
        @pl.when(s != j)
        def _():
            map_copy(0, s, w).wait_recv()

    first = jnp.where(zh == 0, 1.0, 0.0)
    ent[0] = jnp.concatenate([prior[...] * first, jnp.zeros((D, D), F32)], axis=1)
    mul[0] = jnp.ones((8, D), F32)

    def link(i, _):
        m16 = maps[i, 0:C, 0:D]
        add = maps[i, 0:C, D : 2 * D].astype(F32) + maps[i, 0:C, 2 * D : 3 * D].astype(F32)
        ar = maps[i, C : C + 16, :].astype(F32)
        a = (ar[0:8, 0:D] + ar[0:8, D : 2 * D]) + ar[0:8, 2 * D : 3 * D]
        x = ent[i]
        xh, xl = split(x[:, :D])
        mx = dot(m16, jnp.concatenate([xh, xl, x[:, D:].astype(BF16)], axis=1))
        acc = mul[i]
        a1 = a[0:1, :]
        r = a1 * x[:, :D] + (mx[:, :D] + mx[:, D : 2 * D]) + add
        p = a1 * x[:, D:] + mx[:, 2 * D :] + acc[0:1, :] * m16.astype(F32)
        ent[i + 1] = jnp.concatenate([r, p], axis=1)
        mul[i + 1] = a * acc
        return 0

    lax.fori_loop(0, HALF, link, 0)

    def z_copy(src, dst, i, to):
        return remote(src, dst, z_s.at[i], z_r.at[i], to)

    last = ent.at[HALF]
    to_one = [z_copy(last.at[:, pl.ds(0, D)], mid, 0, j + HALF)]
    to_zero = [
        z_copy(last, fin_z, 1, j),
        z_copy(mul.at[HALF], mul.at[HALF + 1], 2, j),
    ]

    def send_sin():
        for d in range(1, HALF):
            sin_copies[d - 1].start()

    sin_copies = [
        remote(
            sin16.at[(j + d) % HALF], sin.at[j], sin_s.at[d], sin_r.at[d],
            zh * HALF + (j + d) % HALF,
        )
        for d in range(1, HALF)
    ]
    fin_copies = [
        remote(finp, fin.at[j], fin_s.at[d], fin_r.at[d], zh * HALF + (j + d) % HALF)
        for d in range(1, HALF)
    ]

    @pl.when(zh == 0)
    def _():
        for copy in to_one:
            copy.start()

        def stage(i, _):
            sin16[i] = ent[i, :, 0:D].astype(BF16)
            return 0

        lax.fori_loop(0, HALF, stage, 0)
        send_sin()

    @pl.when(zh == 1)
    def _():
        for copy in to_zero:
            copy.start()

    for copy in att_copies:
        copy.wait()
    for i in range(4):
        own_k[2 * i : 2 * i + 2, :] = ak_ref[0, i].astype(F32)
    own = dot_nt(own_q[...], own_k[...].astype(BF16)) * (256**-0.5)
    r = lax.broadcasted_iota(jnp.int32, (16, 8), 0) // 4
    cc = lax.broadcasted_iota(jnp.int32, (16, 8), 1)
    own = jnp.where((cc % 2 == group) & (cc // 2 <= r), own, NEG)
    top = jnp.max(own, axis=1, keepdims=True)
    levels = []
    for s in range(WIDE):
        pk = parts[s, 16:32, :].astype(F32)
        lv = (pk[:, 0:1] + pk[:, 64:65]) + pk[:, 128:129]
        levels.append(lv)
        top = jnp.maximum(top, lv)
    pw = jnp.exp(own - top).astype(BF16)
    den = jnp.sum(pw.astype(F32), axis=1, keepdims=True)
    for i in range(4):
        own_k[2 * i : 2 * i + 2, :] = av_ref[0, i].astype(F32)
    num = dot(pw, own_k[...].astype(BF16))
    for s in range(WIDE):
        wt = jnp.exp(levels[s] - top)
        den = den + wt
        num = num + wt * parts[s, 0:16, :].astype(F32)
    for i in range(4):
        a0s[4 * i : 4 * i + 4, :] = ag_ref[0, i].astype(F32)
    done = num / den * sigmoid(a0s[...])
    for half in range(2):
        a1s[...] = done[:, half * 128 : (half + 1) * 128]
        for h in range(4):
            at = h * 256 + half * 128
            att_ref[0, :, at : at + 128] = a1s[pl.ds(h, 4, stride=4), :].astype(BF16)

    gain = gain_ref[...]
    vf[...] = gv[...].astype(F32)

    @pl.when(zh == 1)
    def _():
        to_one[0].wait_recv()
        s = mid[...]
        sh, sl = split(s)
        both = jnp.concatenate([sh, sl], axis=1)

        def enter(i, _):
            x = ent[i]
            y = dot(x[:, D:].astype(BF16), both)
            sin16[i] = (x[:, :D] + mul[i, 0:1, :] * s + (y[:, :D] + y[:, D:])).astype(BF16)
            return 0

        lax.fori_loop(0, HALF + 1, enter, 0)
        send_sin()
        finp[...] = sin16[HALF]

    @pl.when(zh == 0)
    def _():
        for copy in to_zero:
            copy.wait_recv()
        s = ent[HALF, :, 0:D]
        sh, sl = split(s)
        x = fin_z[...]
        y = dot(x[:, D:].astype(BF16), jnp.concatenate([sh, sl], axis=1))
        finp[...] = (
            x[:, :D] + mul[HALF + 1, 0:1, :] * s + (y[:, :D] + y[:, D:])
        ).astype(BF16)

    for copy in fin_copies:
        copy.start()
    fin[j] = finp[...]
    sin[j] = sin16[j]
    for copy in sin_copies:
        copy.wait()

    def finish(h, _):
        s = sin[h]
        o = o0[h] + dot(gq[h], jnp.concatenate([s, s], axis=0))
        scale = lax.rsqrt(jnp.mean(o * o, axis=1, keepdims=True) + EPS)
        z = vf[pl.ds(h, TOK, stride=HEADS), :]
        r = (o * scale * gain * (z * sigmoid(z))).astype(BF16)
        out_ref[:, pl.ds(pl.multiple_of(h * D, D), D)] = r
        return 0

    lax.fori_loop(0, HEADS, finish, 0)

    kraw, qraw = [], []
    for i in range(4):
        for ref, at, keep in ((sk_ref, 0, kraw), (sq_ref, 4, qraw)):
            x = ref[0, i].astype(F32)
            kqs[pl.ds(at + i, KHEADS, stride=8), :] = x
            uscr[pl.ds(0, KHEADS, stride=2), :] = x
            uscr[pl.ds(1, KHEADS, stride=2), :] = x
            keep.append(uscr[0:HEADS, :])
    rk = [lax.rsqrt(jnp.sum(x * x, axis=1, keepdims=True) + EPS) for x in kraw]
    rq = [lax.rsqrt(jnp.sum(x * x, axis=1, keepdims=True) + EPS) * (D**-0.5) for x in qraw]
    kn = [x * r for x, r in zip(kraw, rk)]
    qn = [x * r for x, r in zip(qraw, rq)]
    diag = lax.broadcasted_iota(jnp.int32, (HEADS, HEADS), 0) == lax.broadcasted_iota(
        jnp.int32, (HEADS, HEADS), 1
    )

    def column(x):
        return jnp.sum(jnp.where(diag, x, 0.0), axis=1, keepdims=True)

    sb = sigmoid(sb_ref[0])
    sd = sd_ref[0]
    beta = [column(sb[i : i + 1, :]) for i in range(4)]
    cum = [column(sd[0:1, :])]
    for i in range(1, 4):
        cum.append(cum[-1] + column(sd[i : i + 1, :]))
    for copy in fin_copies:
        copy.wait()
    for h in range(HEADS):
        kh = h // 2
        res[h * 8 : (h + 1) * 8, :] = dot(kqs[kh * 8 : (kh + 1) * 8, :].astype(BF16), fin[h])
    us = []
    for i in range(4):
        ks = res[pl.ds(i, HEADS, stride=8), :] * (rk[i] * jnp.exp(cum[i]))
        u = sv_ref[0, i].astype(F32) - ks
        for p in range(i):
            kk = jnp.sum(kn[i] * kn[p], axis=1, keepdims=True)
            u = u - (jnp.exp(cum[i] - cum[p]) * kk) * us[p]
        u = beta[i] * u
        us.append(u)
        o = res[pl.ds(4 + i, HEADS, stride=8), :] * (rq[i] * jnp.exp(cum[i]))
        for p in range(i + 1):
            qk = jnp.sum(qn[i] * kn[p], axis=1, keepdims=True)
            o = o + (jnp.exp(cum[i] - cum[p]) * qk) * us[p]
        scale = lax.rsqrt(jnp.mean(o * o, axis=1, keepdims=True) + EPS)
        z = sg_ref[0, i].astype(F32)
        sscr[i * 8 : (i + 1) * 8, :] = o * scale * gain * (z * sigmoid(z))
    for h in range(HEADS):
        step_ref[0, :, h * D : (h + 1) * D] = sscr[pl.ds(h, 4, stride=8), :].astype(BF16)
    for i in range(4):
        uscr[pl.ds(i, HEADS, stride=8), :] = us[i] * (jnp.exp(cum[3] - cum[i]) * rk[i])
        uscr[pl.ds(4 + i, HEADS, stride=8), :] = jnp.zeros((HEADS, D), F32)
    decay = jnp.broadcast_to(jnp.exp(cum[3]), (HEADS, D))
    for h in range(HEADS):
        kh = h // 2
        uh, ul = split(uscr[h * 8 : (h + 1) * 8, :])
        y = dot_tn(
            kqs[kh * 8 : (kh + 1) * 8, :].astype(BF16), jnp.concatenate([uh, ul], axis=1)
        )
        state_ref[0, h] = decay[h : h + 1, :] * fin[h].astype(F32) + (y[:, :D] + y[:, D:])

    for hd in range(HALF):
        @pl.when(hd != j)
        def _():
            map_copy(hd, 0, w).wait_send()

    @pl.when(zh == 0)
    def _():
        to_one[0].wait_send()

    @pl.when(zh == 1)
    def _():
        for copy in to_zero:
            copy.wait_send()


def shards(
    span_query, span_key, span_value, span_beta_logit, span_logdecay, span_gate,
    norm_gain, prior_state,
    step_query, step_key, step_value, step_beta_logit, step_logdecay, step_gate,
    cache_key, cache_value, att_query, att_key, att_value, att_gate,
):
    def rows(c):
        return c.reshape(2048, 2, 2, 128).transpose(0, 2, 1, 3).reshape(8192, 128)

    vm = pl.BlockSpec(memory_space=pltpu.VMEM)
    hbm = pl.BlockSpec(memory_space=pltpu.HBM)
    sem = pltpu.SemaphoreType.DMA
    V = pltpu.VMEM
    return pl.pallas_call(
        kernel,
        out_shape=(
            jax.ShapeDtypeStruct((TOK, HEADS * D), BF16),
            jax.ShapeDtypeStruct((1, 4, HEADS * D), BF16),
            jax.ShapeDtypeStruct((1, HEADS, D, D), F32),
            jax.ShapeDtypeStruct((1, 4, 1024), BF16),
        ),
        in_specs=[hbm, hbm, hbm, vm, vm, hbm, vm, hbm] + [vm] * 6 + [hbm, hbm] + [vm] * 4,
        out_specs=(vm,) * 4,
        scratch_shapes=[
            V((TOK * KHEADS, D), BF16), V((TOK * KHEADS, D), BF16), V((TOK * HEADS, D), BF16),
            V((TOK * HEADS, D), BF16), V((8192, D), BF16), V((8192, D), BF16), V((D, D), F32),
            V((TOK * KHEADS, D), F32), V((TOK * KHEADS, D), F32), V((TOK * HEADS, D), F32),
            V((8192, D), F32), V((2048, 256), BF16), V((2048, 256), BF16), V((256, 2048), F32),
            V((KHEADS, 8, TOK), F32),
            V((HEADS, C + 16, 3 * D), BF16), V((HALF, C + 16, 3 * D), BF16),
            V((HEADS, TOK, D), F32), V((HEADS, TOK, 2 * D), BF16),
            V((HALF + 1, D, 2 * D), F32), V((HALF + 2, 8, D), F32), V((D, D), F32),
            V((D, 2 * D), F32),
            V((HALF + 1, D, D), BF16), V((HALF, D, D), BF16), V((D, D), BF16),
            V((HALF, D, D), BF16),
            V((16, 256), BF16), V((WIDE, 16, 256), BF16),
            V((WIDE, 32, 256), BF16), V((WIDE, 32, 256), BF16),
            V((32, D), F32), V((64, D), F32), V((64, D), F32), V((32, D), F32),
            V((16, 256), F32), V((16, D), F32), V((8, 256), F32),
            sem((8,)), sem((WIDE,)), sem((WIDE,)), sem((WIDE,)), sem((WIDE,)),
            sem((HALF,)), sem((HALF,)), sem((HALF,)), sem((HALF,)), sem((HALF,)), sem((HALF,)),
            sem((3,)), sem((3,)),
        ],
        compiler_params=pltpu.CompilerParams(
            collective_id=0, has_side_effects=True, vmem_limit_bytes=56 * 2**20
        ),
        name="rollout_fork",
    )(
        span_query.reshape(TOK * KHEADS, D), span_key.reshape(TOK * KHEADS, D),
        span_value.reshape(TOK * HEADS, D), span_beta_logit.T, span_logdecay.T,
        span_gate.reshape(TOK * HEADS, D), norm_gain.reshape(1, D), prior_state,
        step_query, step_key, step_value, step_beta_logit, step_logdecay, step_gate,
        rows(cache_key), rows(cache_value), att_query, att_key, att_value, att_gate,
    )


def solution(mesh):
    tok = P(("prompt", "wide"), "tp", None)
    tok2 = P(("prompt", "wide"), "tp")
    stp = P(("prompt", "wide"), None, "tp", None)
    stp2 = P(("prompt", "wide"), None, "tp")
    in_specs = (
        tok, tok, tok, tok2, tok2, tok, P(), P(("prompt", "tp"), None, None),
        stp, stp, stp, stp2, stp2, stp,
        P(("prompt", "wide"), None, None), P(("prompt", "wide"), None, None),
        stp, P(("prompt", "wide"), None, None, None), P(("prompt", "wide"), None, None, None), stp,
    )
    out_specs = (
        P(("prompt", "wide"), "tp"),
        stp2,
        P(("prompt", "wide"), "tp", None, None),
        stp2,
    )
    return jax.shard_map(shards, mesh=mesh, in_specs=in_specs, out_specs=out_specs, check_vma=False)
```

```python
import jax
import jax.numpy as jnp
from jax import lax
from jax.experimental import pallas as pl
from jax.experimental.pallas import tpu as pltpu
from jax.sharding import PartitionSpec as P

F32 = jnp.float32
BF16 = jnp.bfloat16
MESH = pl.DeviceIdType.MESH
EPS = 1e-6
C = 128
D = 128
HEADS = 8
KHEADS = 4
TOK = 512
NCH = TOK // C
HALF = 8
WIDE = 16
NEG = -1e30


def dot(a, b):
    return lax.dot_general(a, b, (((1,), (0,)), ((), ())), preferred_element_type=F32)


def dot_nt(a, b):
    return lax.dot_general(a, b, (((1,), (1,)), ((), ())), preferred_element_type=F32)


def dot_tn(a, b):
    return lax.dot_general(a, b, (((0,), (0,)), ((), ())), preferred_element_type=F32)


def split(x):
    hi = x.astype(BF16)
    return hi, (x - hi.astype(F32)).astype(BF16)


def sigmoid(x):
    return 1.0 / (1.0 + jnp.exp(-x))


def kernel(
    q_hbm, k_hbm, v_hbm, bl_ref, ld_ref, gate_hbm, gain_ref, prior_hbm,
    sq_ref, sk_ref, sv_ref, sb_ref, sd_ref, sg_ref,
    ck_hbm, cv_hbm, aq_ref, ak_ref, av_ref, ag_ref,
    out_ref, step_ref, state_ref, att_ref,
    qv, kv, vv, gv, ckv, cvv, prior,
    qf, kf, vf, cf, kc, vc, scores, scal,
    wire, maps, o0, gq, ent, mul, mid, fin_z, out_z,
    sin16, sin, finp, fin, own_q, all_q, msg, parts,
    kqs, res, uscr, sscr, a0s, a1s, own_k,
    load, q_s, q_r, att_s, att_r, map_s, map_r, sin_s, sin_r, fin_s, fin_r, z_s, z_r,
):
    w = lax.axis_index("wide")
    zh = w // HALF
    j = w % HALF
    group = lax.axis_index("tp") // 2

    loads = []
    for i, (src, dst) in enumerate((
        (q_hbm, qv), (k_hbm, kv), (v_hbm, vv), (ck_hbm, ckv), (cv_hbm, cvv), (gate_hbm, gv),
        (prior_hbm.at[j], prior),
    )):
        copy = pltpu.make_async_copy(src, dst, load.at[i])
        copy.start()
        loads.append(copy)

    barrier = pltpu.get_barrier_semaphore()
    for d in range(1, WIDE):
        pl.semaphore_signal(
            barrier, inc=1, device_id={"wide": (w + d) % WIDE}, device_id_type=MESH
        )
    for i in range(4):
        a0s[4 * i : 4 * i + 4, :] = aq_ref[0, i].astype(F32)
    own_q[...] = a0s[...].astype(BF16)
    upper = (
        lax.broadcasted_iota(jnp.int32, (C, C), 0) <= lax.broadcasted_iota(jnp.int32, (C, C), 1)
    ).astype(F32)
    scal[...] = jnp.zeros_like(scal)
    for c in range(NCH):
        part = slice(c * C, (c + 1) * C)
        g8 = lax.dot_general(
            ld_ref[:, part], upper, (((1,), (0,)), ((), ())),
            precision=lax.Precision.HIGHEST, preferred_element_type=F32,
        )
        b8 = sigmoid(bl_ref[:, part])
        for kh in range(KHEADS):
            scal[kh, 0:2, part] = g8[2 * kh : 2 * kh + 2]
            scal[kh, 2:4, part] = b8[2 * kh : 2 * kh + 2]

    for copy in loads[:3]:
        copy.wait()
    qf[...] = qv[...].astype(F32)
    kf[...] = kv[...].astype(F32)
    vf[...] = vv[...].astype(F32)
    pl.semaphore_wait(barrier, WIDE - 1)

    def remote(src, dst, ss, rs, to):
        return pltpu.make_async_remote_copy(
            src_ref=src, dst_ref=dst, send_sem=ss, recv_sem=rs,
            device_id={"wide": to}, device_id_type=MESH,
        )

    def map_copy(to, slot, device):
        return remote(wire.at[to], maps.at[slot], map_s.at[to], map_r.at[slot], device)

    q_copies = []
    for d in range(1, WIDE):
        copy = remote(own_q, all_q.at[w], q_s.at[d], q_r.at[d], (w + d) % WIDE)
        copy.start()
        q_copies.append(copy)
    all_q[w] = own_q[...]

    att_copies = []
    for d in range(1, WIDE):
        to = (w + d) % WIDE
        att_copies.append(remote(msg.at[to], parts.at[w], att_s.at[d], att_r.at[d], to))

    def attend():
        for load_copy, raw, cut in ((loads[3], ckv, kc), (loads[4], cvv, vc)):
            load_copy.wait()
            cf[...] = raw[...].astype(F32)
            cut[:, 0:128] = cf[pl.ds(group, 2048, stride=4), :].astype(BF16)
            cut[:, 128:256] = cf[pl.ds(2 + group, 2048, stride=4), :].astype(BF16)
        for copy in q_copies:
            copy.wait()
        scores[...] = dot_nt(all_q[...].reshape(256, 256), kc[...]) * (256**-0.5)
        sc = scores[...]
        top = jnp.max(sc, axis=1, keepdims=True)
        wt = jnp.exp(sc - top).astype(BF16)
        total = jnp.sum(wt.astype(F32), axis=1, keepdims=True)
        num = (dot(wt, vc[...]) / total).astype(BF16)
        level = top + jnp.log(total)
        l0 = level.astype(BF16).astype(F32)
        l1 = (level - l0).astype(BF16).astype(F32)
        l2 = level - l0 - l1
        lane = lax.broadcasted_iota(jnp.int32, (256, 256), 1)
        packed = jnp.where(lane < 64, l0, jnp.where(lane < 128, l1, l2)).astype(BF16)
        for s in range(WIDE):
            msg[s, 0:16, :] = num[s * 16 : (s + 1) * 16, :]
            msg[s, 16:32, :] = packed[s * 16 : (s + 1) * 16, :]
        for copy in att_copies:
            copy.start()
        parts[w] = msg[w]

    row = lax.broadcasted_iota(jnp.int32, (C, C), 0)
    col = lax.broadcasted_iota(jnp.int32, (C, C), 1)

    def head(it, _):
        kh = (j // 2 + jnp.where(it == 0, 2, 0) + jnp.where(it == 1, 1, 0)
              + jnp.where(it == 2, 3, 0)) % KHEADS

        @pl.when(it == 1)
        def _():
            attend()

        ks, qs, kts, cells = [], [], [], []
        for c in range(NCH):
            k32 = kf[pl.ds(c * C * KHEADS + kh, C, stride=KHEADS), :]
            q32 = qf[pl.ds(c * C * KHEADS + kh, C, stride=KHEADS), :]
            k16 = k32.astype(BF16)
            q16 = q32.astype(BF16)
            kt16 = k32.T.astype(BF16)
            kq = dot(jnp.concatenate([k16, q16], axis=0), kt16)
            kk, qk = kq[:C], kq[C:]
            eye = jnp.where(row == col, kk, 0.0)
            rk_row = lax.rsqrt(jnp.sum(eye, axis=0, keepdims=True) + EPS)
            rk = lax.rsqrt(jnp.sum(k32 * k32, axis=1, keepdims=True) + EPS)
            rq = lax.rsqrt(jnp.sum(q32 * q32, axis=1, keepdims=True) + EPS) * (D**-0.5)
            kkn = kk * rk * rk_row
            qkn = qk * rq * rk_row
            g_rows = scal[kh, :, c * C : (c + 1) * C]
            cols = g_rows.T
            for e in range(2):
                g_row = g_rows[e : e + 1, :]
                g = cols[:, e : e + 1]
                b = cols[:, 2 + e : 3 + e]
                ratio = jnp.exp(jnp.where(row >= col, g - g_row, NEG))
                low = jnp.where(row > col, ratio * kkn * b, 0.0)
                eg = jnp.exp(g)
                g_end = g[C - 1 : C, :]
                v32 = vf[pl.ds(c * C * HEADS + 2 * kh + e, C, stride=HEADS), :]
                cells.append(dict(
                    low=low, sc=split(ratio * qkn), egq=eg * rq, e_end=jnp.exp(g_end),
                    out=jnp.exp(g_end - g) * rk,
                    rhs=jnp.concatenate([b * v32, (b * eg * rk) * k32], axis=1),
                ))
            qs.append((q32, q16))
            kts.append(kt16)
        invs = [-jnp.where((row >> 1) == (col >> 1), x["low"], 0.0) for x in cells]
        for lg in range(1, 7):
            here = ((row >> (lg + 1)) == (col >> (lg + 1))) & ((row >> lg) != (col >> lg))
            offs = [jnp.where(here, x["low"], 0.0) for x in cells]
            i16 = [x.astype(BF16) for x in invs]
            ys = [o + dot(i, o.astype(BF16)) for o, i in zip(offs, i16)]
            zs = [dot(y.astype(BF16), i) for y, i in zip(ys, i16)]
            invs = [v - (y + z) for v, y, z in zip(invs, ys, zs)]
        xs = [x["rhs"] + dot(i.astype(BF16), x["rhs"].astype(BF16)) for x, i in zip(cells, invs)]
        adds = []
        for c in range(NCH):
            kt2 = jnp.concatenate([kts[c], kts[c]], axis=1)
            for e in range(2):
                i = 2 * c + e
                h, l = split(cells[i]["out"] * xs[i])
                adds.append(dot(kt2, jnp.concatenate([h, l], axis=0)))
        rps, accs = [[None, None]], [[None, None]]
        for c in range(NCH):
            nrp, nacc = [], []
            for e in range(2):
                i = 2 * c + e
                e_end = cells[i]["e_end"]
                inc, neg = adds[i][:, :D], -adds[i][:, D:]
                if c == 0:
                    nrp.append(jnp.concatenate([inc, neg], axis=1))
                    nacc.append(e_end)
                else:
                    old, acc = rps[c][e], accs[c][e]
                    nrp.append(
                        e_end * old + jnp.concatenate([inc, acc * neg], axis=1)
                        + dot(neg.astype(BF16), old.astype(BF16))
                    )
                    nacc.append(e_end * acc)
            rps.append(nrp)
            accs.append(nacc)
        rp, acc = rps[NCH], accs[NCH]
        for e in range(2):
            hd = 2 * kh + e
            bh, bl = split(rp[e][:, :D])
            wire[hd, 0:C, 0:D] = rp[e][:, D:].astype(BF16)
            wire[hd, 0:C, D : 2 * D] = bh
            wire[hd, 0:C, 2 * D : 3 * D] = bl
            a = jnp.broadcast_to(acc[e], (16, 3 * D))
            a0 = a.astype(BF16).astype(F32)
            a1 = (a - a0).astype(BF16).astype(F32)
            a2 = a - a0 - a1
            lane = lax.broadcasted_iota(jnp.int32, (16, 3 * D), 1)
            wire[hd, C : C + 16, :] = jnp.where(
                lane < D, a0, jnp.where(lane < 2 * D, a1, a2)
            ).astype(BF16)

            @pl.when(hd == j)
            def _():
                maps[j] = wire[hd]

            @pl.when(hd != j)
            def _():
                map_copy(hd, j, zh * HALF + hd).start()
        for c in range(NCH):
            q32, q16 = qs[c]
            for e in range(2):
                hd = 2 * kh + e
                x = xs[2 * c + e]
                cell = cells[2 * c + e]
                if c == 0:
                    uw = jnp.concatenate([x[:, :D], -x[:, D:]], axis=1)
                else:
                    rp16 = rps[c][e].astype(BF16)
                    p = dot(x[:, D:].astype(BF16), rp16)
                    uw = jnp.concatenate(
                        [x[:, :D] - p[:, :D], -(accs[c][e] * x[:, D:] + p[:, D:])], axis=1
                    )
                uh, ul = split(uw)
                sch, scl = cell["sc"]
                og = dot(
                    jnp.concatenate([sch, scl, sch], axis=1),
                    jnp.concatenate([uh, uh, ul], axis=0),
                )
                direct = cell["egq"]
                if c > 0:
                    og = og + direct * dot(q16, rp16)
                    direct = direct * accs[c][e]
                o0[hd, c * C : (c + 1) * C, :] = og[:, :D]
                gh, gl = split(og[:, D:] + direct * q32)
                gq[hd, c * C : (c + 1) * C, :D] = gh
                gq[hd, c * C : (c + 1) * C, D:] = gl
        return 0

    lax.fori_loop(0, KHEADS, head, 0)
    for copy in loads[5:]:
        copy.wait()

    for s in range(HALF):
        @pl.when(s != j)
        def _():
            map_copy(0, s, w).wait_recv()

    first = jnp.where(zh == 0, 1.0, 0.0)
    ent[0] = jnp.concatenate([prior[...] * first, jnp.zeros((D, D), F32)], axis=1)
    mul[0] = jnp.ones((8, D), F32)

    def link(i, _):
        m16 = maps[i, 0:C, 0:D]
        add = maps[i, 0:C, D : 2 * D].astype(F32) + maps[i, 0:C, 2 * D : 3 * D].astype(F32)
        ar = maps[i, C : C + 16, :].astype(F32)
        a = (ar[0:8, 0:D] + ar[0:8, D : 2 * D]) + ar[0:8, 2 * D : 3 * D]
        x = ent[i]
        xh, xl = split(x[:, :D])
        mx = dot(m16, jnp.concatenate([xh, xl, x[:, D:].astype(BF16)], axis=1))
        acc = mul[i]
        a1 = a[0:1, :]
        r = a1 * x[:, :D] + (mx[:, :D] + mx[:, D : 2 * D]) + add
        p = a1 * x[:, D:] + mx[:, 2 * D :] + acc[0:1, :] * m16.astype(F32)
        ent[i + 1] = jnp.concatenate([r, p], axis=1)
        mul[i + 1] = a * acc
        return 0

    lax.fori_loop(0, HALF, link, 0)

    def z_copy(src, dst, i, to):
        return remote(src, dst, z_s.at[i], z_r.at[i], to)

    out_z[...] = ent[HALF].astype(BF16)
    to_one = [z_copy(out_z.at[:, pl.ds(0, D)], mid, 0, j + HALF)]
    to_zero = [
        z_copy(out_z, fin_z, 1, j),
        z_copy(mul.at[HALF], mul.at[HALF + 1], 2, j),
    ]

    def send_sin():
        for d in range(1, HALF):
            sin_copies[d - 1].start()

    sin_copies = [
        remote(
            sin16.at[(j + d) % HALF], sin.at[j], sin_s.at[d], sin_r.at[d],
            zh * HALF + (j + d) % HALF,
        )
        for d in range(1, HALF)
    ]
    fin_copies = [
        remote(finp, fin.at[j], fin_s.at[d], fin_r.at[d], zh * HALF + (j + d) % HALF)
        for d in range(1, HALF)
    ]

    @pl.when(zh == 0)
    def _():
        for copy in to_one:
            copy.start()

        def stage(i, _):
            sin16[i] = ent[i, :, 0:D].astype(BF16)
            return 0

        lax.fori_loop(0, HALF, stage, 0)
        send_sin()

    @pl.when(zh == 1)
    def _():
        for copy in to_zero:
            copy.start()

    for copy in att_copies:
        copy.wait()
    for i in range(4):
        own_k[2 * i : 2 * i + 2, :] = ak_ref[0, i].astype(F32)
    own = dot_nt(own_q[...], own_k[...].astype(BF16)) * (256**-0.5)
    r = lax.broadcasted_iota(jnp.int32, (16, 8), 0) // 4
    cc = lax.broadcasted_iota(jnp.int32, (16, 8), 1)
    own = jnp.where((cc % 2 == group) & (cc // 2 <= r), own, NEG)
    top = jnp.max(own, axis=1, keepdims=True)
    levels = []
    for s in range(WIDE):
        pk = parts[s, 16:32, :].astype(F32)
        lv = (pk[:, 0:1] + pk[:, 64:65]) + pk[:, 128:129]
        levels.append(lv)
        top = jnp.maximum(top, lv)
    pw = jnp.exp(own - top).astype(BF16)
    den = jnp.sum(pw.astype(F32), axis=1, keepdims=True)
    for i in range(4):
        own_k[2 * i : 2 * i + 2, :] = av_ref[0, i].astype(F32)
    num = dot(pw, own_k[...].astype(BF16))
    for s in range(WIDE):
        wt = jnp.exp(levels[s] - top)
        den = den + wt
        num = num + wt * parts[s, 0:16, :].astype(F32)
    for i in range(4):
        a0s[4 * i : 4 * i + 4, :] = ag_ref[0, i].astype(F32)
    done = num / den * sigmoid(a0s[...])
    for half in range(2):
        a1s[...] = done[:, half * 128 : (half + 1) * 128]
        for h in range(4):
            at = h * 256 + half * 128
            att_ref[0, :, at : at + 128] = a1s[pl.ds(h, 4, stride=4), :].astype(BF16)

    gain = gain_ref[...]
    vf[...] = gv[...].astype(F32)

    @pl.when(zh == 1)
    def _():
        to_one[0].wait_recv()
        s16 = mid[...]
        s32 = s16.astype(F32)

        def enter(i):
            x = ent[i]
            y = dot(x[:, D:].astype(BF16), s16)
            return (x[:, :D] + mul[i, 0:1, :] * s32 + y).astype(BF16)

        for d in range(1, HALF):
            to = (j + d) % HALF
            sin16[to] = enter(to)
            sin_copies[d - 1].start()
        finp[...] = enter(HALF)
        sin16[j] = enter(j)

    @pl.when(zh == 0)
    def _():
        for copy in to_zero:
            copy.wait_recv()
        s = ent[HALF, :, 0:D]
        sh, sl = split(s)
        x = fin_z[...]
        y = dot(x[:, D:], jnp.concatenate([sh, sl], axis=1))
        finp[...] = (
            x[:, :D].astype(F32) + mul[HALF + 1, 0:1, :] * s + (y[:, :D] + y[:, D:])
        ).astype(BF16)

    for copy in fin_copies:
        copy.start()
    fin[j] = finp[...]
    sin[j] = sin16[j]
    for copy in sin_copies:
        copy.wait()

    def finish(h, _):
        s = sin[h]
        o = o0[h] + dot(gq[h], jnp.concatenate([s, s], axis=0))
        scale = lax.rsqrt(jnp.mean(o * o, axis=1, keepdims=True) + EPS)
        z = vf[pl.ds(h, TOK, stride=HEADS), :]
        r = (o * scale * gain * (z * sigmoid(z))).astype(BF16)
        out_ref[:, pl.ds(pl.multiple_of(h * D, D), D)] = r
        return 0

    lax.fori_loop(0, HEADS, finish, 0)

    kraw, qraw = [], []
    for i in range(4):
        for ref, at, keep in ((sk_ref, 0, kraw), (sq_ref, 4, qraw)):
            x = ref[0, i].astype(F32)
            kqs[pl.ds(at + i, KHEADS, stride=8), :] = x
            uscr[pl.ds(0, KHEADS, stride=2), :] = x
            uscr[pl.ds(1, KHEADS, stride=2), :] = x
            keep.append(uscr[0:HEADS, :])
    rk = [lax.rsqrt(jnp.sum(x * x, axis=1, keepdims=True) + EPS) for x in kraw]
    rq = [lax.rsqrt(jnp.sum(x * x, axis=1, keepdims=True) + EPS) * (D**-0.5) for x in qraw]
    kn = [x * r for x, r in zip(kraw, rk)]
    qn = [x * r for x, r in zip(qraw, rq)]
    diag = lax.broadcasted_iota(jnp.int32, (HEADS, HEADS), 0) == lax.broadcasted_iota(
        jnp.int32, (HEADS, HEADS), 1
    )

    def column(x):
        return jnp.sum(jnp.where(diag, x, 0.0), axis=1, keepdims=True)

    sb = sigmoid(sb_ref[0])
    sd = sd_ref[0]
    beta = [column(sb[i : i + 1, :]) for i in range(4)]
    cum = [column(sd[0:1, :])]
    for i in range(1, 4):
        cum.append(cum[-1] + column(sd[i : i + 1, :]))
    for copy in fin_copies:
        copy.wait()
    for h in range(HEADS):
        kh = h // 2
        res[h * 8 : (h + 1) * 8, :] = dot(kqs[kh * 8 : (kh + 1) * 8, :].astype(BF16), fin[h])
    us = []
    for i in range(4):
        ks = res[pl.ds(i, HEADS, stride=8), :] * (rk[i] * jnp.exp(cum[i]))
        u = sv_ref[0, i].astype(F32) - ks
        for p in range(i):
            kk = jnp.sum(kn[i] * kn[p], axis=1, keepdims=True)
            u = u - (jnp.exp(cum[i] - cum[p]) * kk) * us[p]
        u = beta[i] * u
        us.append(u)
        o = res[pl.ds(4 + i, HEADS, stride=8), :] * (rq[i] * jnp.exp(cum[i]))
        for p in range(i + 1):
            qk = jnp.sum(qn[i] * kn[p], axis=1, keepdims=True)
            o = o + (jnp.exp(cum[i] - cum[p]) * qk) * us[p]
        scale = lax.rsqrt(jnp.mean(o * o, axis=1, keepdims=True) + EPS)
        z = sg_ref[0, i].astype(F32)
        sscr[i * 8 : (i + 1) * 8, :] = o * scale * gain * (z * sigmoid(z))
    for h in range(HEADS):
        step_ref[0, :, h * D : (h + 1) * D] = sscr[pl.ds(h, 4, stride=8), :].astype(BF16)
    for i in range(4):
        uscr[pl.ds(i, HEADS, stride=8), :] = us[i] * (jnp.exp(cum[3] - cum[i]) * rk[i])
        uscr[pl.ds(4 + i, HEADS, stride=8), :] = jnp.zeros((HEADS, D), F32)
    decay = jnp.broadcast_to(jnp.exp(cum[3]), (HEADS, D))
    for h in range(HEADS):
        kh = h // 2
        uh, ul = split(uscr[h * 8 : (h + 1) * 8, :])
        y = dot_tn(
            kqs[kh * 8 : (kh + 1) * 8, :].astype(BF16), jnp.concatenate([uh, ul], axis=1)
        )
        state_ref[0, h] = decay[h : h + 1, :] * fin[h].astype(F32) + (y[:, :D] + y[:, D:])

    for hd in range(HALF):
        @pl.when(hd != j)
        def _():
            map_copy(hd, 0, w).wait_send()

    @pl.when(zh == 0)
    def _():
        to_one[0].wait_send()

    @pl.when(zh == 1)
    def _():
        for copy in to_zero:
            copy.wait_send()


def hand_out(a, b, c, d, ao, bo, co, do):
    for src, dst in ((a, ao), (b, bo), (c, co), (d, do)):
        dst[...] = src[...]


def shards(
    span_query, span_key, span_value, span_beta_logit, span_logdecay, span_gate,
    norm_gain, prior_state,
    step_query, step_key, step_value, step_beta_logit, step_logdecay, step_gate,
    cache_key, cache_value, att_query, att_key, att_value, att_gate,
):
    def rows(c):
        return c.reshape(2048, 2, 2, 128).transpose(0, 2, 1, 3).reshape(8192, 128)

    vm = pl.BlockSpec(memory_space=pltpu.VMEM)
    hbm = pl.BlockSpec(memory_space=pltpu.HBM)
    sem = pltpu.SemaphoreType.DMA
    V = pltpu.VMEM
    results = pl.pallas_call(
        kernel,
        out_shape=(
            jax.ShapeDtypeStruct((TOK, HEADS * D), BF16),
            jax.ShapeDtypeStruct((1, 4, HEADS * D), BF16),
            jax.ShapeDtypeStruct((1, HEADS, D, D), F32),
            jax.ShapeDtypeStruct((1, 4, 1024), BF16),
        ),
        in_specs=[hbm, hbm, hbm, vm, vm, hbm, vm, hbm] + [vm] * 6 + [hbm, hbm] + [vm] * 4,
        out_specs=(vm,) * 4,
        scratch_shapes=[
            V((TOK * KHEADS, D), BF16), V((TOK * KHEADS, D), BF16), V((TOK * HEADS, D), BF16),
            V((TOK * HEADS, D), BF16), V((8192, D), BF16), V((8192, D), BF16), V((D, D), F32),
            V((TOK * KHEADS, D), F32), V((TOK * KHEADS, D), F32), V((TOK * HEADS, D), F32),
            V((8192, D), F32), V((2048, 256), BF16), V((2048, 256), BF16), V((256, 2048), F32),
            V((KHEADS, 8, TOK), F32),
            V((HEADS, C + 16, 3 * D), BF16), V((HALF, C + 16, 3 * D), BF16),
            V((HEADS, TOK, D), F32), V((HEADS, TOK, 2 * D), BF16),
            V((HALF + 1, D, 2 * D), F32), V((HALF + 2, 8, D), F32), V((D, D), BF16),
            V((D, 2 * D), BF16), V((D, 2 * D), BF16),
            V((HALF + 1, D, D), BF16), V((HALF, D, D), BF16), V((D, D), BF16),
            V((HALF, D, D), BF16),
            V((16, 256), BF16), V((WIDE, 16, 256), BF16),
            V((WIDE, 32, 256), BF16), V((WIDE, 32, 256), BF16),
            V((32, D), F32), V((64, D), F32), V((64, D), F32), V((32, D), F32),
            V((16, 256), F32), V((16, D), F32), V((8, 256), F32),
            sem((8,)), sem((WIDE,)), sem((WIDE,)), sem((WIDE,)), sem((WIDE,)),
            sem((HALF,)), sem((HALF,)), sem((HALF,)), sem((HALF,)), sem((HALF,)), sem((HALF,)),
            sem((3,)), sem((3,)),
        ],
        compiler_params=pltpu.CompilerParams(
            collective_id=0, has_side_effects=True, vmem_limit_bytes=59 * 2**20
        ),
        name="rollout_fork",
    )(
        span_query.reshape(TOK * KHEADS, D), span_key.reshape(TOK * KHEADS, D),
        span_value.reshape(TOK * HEADS, D), span_beta_logit.T, span_logdecay.T,
        span_gate.reshape(TOK * HEADS, D), norm_gain.reshape(1, D), prior_state,
        step_query, step_key, step_value, step_beta_logit, step_logdecay, step_gate,
        rows(cache_key), rows(cache_value), att_query, att_key, att_value, att_gate,
    )
    return pl.pallas_call(
        hand_out,
        out_shape=tuple(jax.ShapeDtypeStruct(x.shape, x.dtype) for x in results),
        in_specs=[vm] * 4,
        out_specs=(vm,) * 4,
        compiler_params=pltpu.CompilerParams(vmem_limit_bytes=8 * 2**20),
        name="hand_out",
    )(*results)


def solution(mesh):
    tok = P(("prompt", "wide"), "tp", None)
    tok2 = P(("prompt", "wide"), "tp")
    stp = P(("prompt", "wide"), None, "tp", None)
    stp2 = P(("prompt", "wide"), None, "tp")
    in_specs = (
        tok, tok, tok, tok2, tok2, tok, P(), P(("prompt", "tp"), None, None),
        stp, stp, stp, stp2, stp2, stp,
        P(("prompt", "wide"), None, None), P(("prompt", "wide"), None, None),
        stp, P(("prompt", "wide"), None, None, None), P(("prompt", "wide"), None, None, None), stp,
    )
    out_specs = (
        P(("prompt", "wide"), "tp"),
        stp2,
        P(("prompt", "wide"), "tp", None, None),
        stp2,
    )
    return jax.shard_map(shards, mesh=mesh, in_specs=in_specs, out_specs=out_specs, check_vma=False)
```

```python
import jax
import jax.numpy as jnp
from jax import lax
from jax.experimental import pallas as pl
from jax.experimental.pallas import tpu as pltpu
from jax.sharding import PartitionSpec as P

F32 = jnp.float32
BF16 = jnp.bfloat16
MESH = pl.DeviceIdType.MESH
EPS = 1e-6
C = 128
D = 128
HEADS = 8
KHEADS = 4
TOK = 512
NCH = TOK // C
HALF = 8
WIDE = 16
NEG = -1e30


def dot(a, b):
    return lax.dot_general(a, b, (((1,), (0,)), ((), ())), preferred_element_type=F32)


def dot_nt(a, b):
    return lax.dot_general(a, b, (((1,), (1,)), ((), ())), preferred_element_type=F32)


def dot_tn(a, b):
    return lax.dot_general(a, b, (((0,), (0,)), ((), ())), preferred_element_type=F32)


def split(x):
    hi = x.astype(BF16)
    return hi, (x - hi.astype(F32)).astype(BF16)


def sigmoid(x):
    return 1.0 / (1.0 + jnp.exp(-x))


def kernel(
    q_hbm, k_hbm, v_hbm, bl_ref, ld_ref, gate_hbm, gain_ref, prior_hbm,
    sq_ref, sk_ref, sv_ref, sb_ref, sd_ref, sg_ref,
    ck_hbm, cv_hbm, aq_ref, ak_ref, av_ref, ag_ref,
    out_ref, step_ref, state_ref, att_ref,
    qv, kv, vv, gv, ckv, cvv, prior,
    qf, kf, vf, cf, kc, vc, scores, scal,
    wire, maps, o0, gq, ent, mul, mid, fin_z, out_z,
    sin16, sin, finp, fin, own_q, all_q, msg, parts,
    kqs, res, uscr, sscr, a0s, a1s, own_k,
    load, q_s, q_r, att_s, att_r, map_s, map_r, sin_s, sin_r, fin_s, fin_r, z_s, z_r,
):
    w = lax.axis_index("wide")
    zh = w // HALF
    j = w % HALF
    group = lax.axis_index("tp") // 2

    loads = []
    for i, (src, dst) in enumerate((
        (q_hbm, qv), (k_hbm, kv), (v_hbm, vv), (ck_hbm, ckv), (cv_hbm, cvv), (gate_hbm, gv),
        (prior_hbm.at[j], prior),
    )):
        copy = pltpu.make_async_copy(src, dst, load.at[i])
        copy.start()
        loads.append(copy)

    barrier = pltpu.get_barrier_semaphore()
    for d in range(1, WIDE):
        pl.semaphore_signal(
            barrier, inc=1, device_id={"wide": (w + d) % WIDE}, device_id_type=MESH
        )
    for i in range(4):
        a0s[4 * i : 4 * i + 4, :] = aq_ref[0, i].astype(F32)
    own_q[...] = a0s[...].astype(BF16)
    upper = (
        lax.broadcasted_iota(jnp.int32, (C, C), 0) <= lax.broadcasted_iota(jnp.int32, (C, C), 1)
    ).astype(F32)
    scal[...] = jnp.zeros_like(scal)
    for c in range(NCH):
        part = slice(c * C, (c + 1) * C)
        g8 = lax.dot_general(
            ld_ref[:, part], upper, (((1,), (0,)), ((), ())),
            precision=lax.Precision.HIGHEST, preferred_element_type=F32,
        )
        b8 = sigmoid(bl_ref[:, part])
        for kh in range(KHEADS):
            scal[kh, 0:2, part] = g8[2 * kh : 2 * kh + 2]
            scal[kh, 2:4, part] = b8[2 * kh : 2 * kh + 2]

    for copy in loads[:3]:
        copy.wait()
    qf[...] = qv[...].astype(F32)
    kf[...] = kv[...].astype(F32)
    vf[...] = vv[...].astype(F32)
    pl.semaphore_wait(barrier, WIDE - 1)

    def remote(src, dst, ss, rs, to):
        return pltpu.make_async_remote_copy(
            src_ref=src, dst_ref=dst, send_sem=ss, recv_sem=rs,
            device_id={"wide": to}, device_id_type=MESH,
        )

    def map_copy(to, slot, device):
        return remote(wire.at[to], maps.at[slot], map_s.at[to], map_r.at[slot], device)

    q_copies = []
    for d in range(1, WIDE):
        copy = remote(own_q, all_q.at[w], q_s.at[d], q_r.at[d], (w + d) % WIDE)
        copy.start()
        q_copies.append(copy)
    all_q[w] = own_q[...]

    att_copies = []
    for d in range(1, WIDE):
        to = (w + d) % WIDE
        att_copies.append(remote(msg.at[to], parts.at[w], att_s.at[d], att_r.at[d], to))

    def attend():
        for load_copy, raw, cut in ((loads[3], ckv, kc), (loads[4], cvv, vc)):
            load_copy.wait()
            cf[...] = raw[...].astype(F32)
            cut[:, 0:128] = cf[pl.ds(group, 2048, stride=4), :].astype(BF16)
            cut[:, 128:256] = cf[pl.ds(2 + group, 2048, stride=4), :].astype(BF16)
        for copy in q_copies:
            copy.wait()
        scores[...] = dot_nt(all_q[...].reshape(256, 256), kc[...]) * (256**-0.5)
        sc = scores[...]
        top = jnp.max(sc, axis=1, keepdims=True)
        wt = jnp.exp(sc - top).astype(BF16)
        total = jnp.sum(wt.astype(F32), axis=1, keepdims=True)
        num = (dot(wt, vc[...]) / total).astype(BF16)
        level = top + jnp.log(total)
        l0 = level.astype(BF16).astype(F32)
        l1 = (level - l0).astype(BF16).astype(F32)
        l2 = level - l0 - l1
        lane = lax.broadcasted_iota(jnp.int32, (256, 256), 1)
        packed = jnp.where(lane < 64, l0, jnp.where(lane < 128, l1, l2)).astype(BF16)
        for s in range(WIDE):
            msg[s, 0:16, :] = num[s * 16 : (s + 1) * 16, :]
            msg[s, 16:32, :] = packed[s * 16 : (s + 1) * 16, :]
        for copy in att_copies:
            copy.start()
        parts[w] = msg[w]

    row = lax.broadcasted_iota(jnp.int32, (C, C), 0)
    col = lax.broadcasted_iota(jnp.int32, (C, C), 1)

    def head(it, _):
        kh = (j // 2 + jnp.where(it == 0, 2, 0) + jnp.where(it == 1, 1, 0)
              + jnp.where(it == 2, 3, 0)) % KHEADS

        @pl.when(it == 1)
        def _():
            attend()

        ks, qs, kts, cells = [], [], [], []
        for c in range(NCH):
            k32 = kf[pl.ds(c * C * KHEADS + kh, C, stride=KHEADS), :]
            q32 = qf[pl.ds(c * C * KHEADS + kh, C, stride=KHEADS), :]
            k16 = k32.astype(BF16)
            q16 = q32.astype(BF16)
            kt16 = k32.T.astype(BF16)
            kq = dot(jnp.concatenate([k16, q16], axis=0), kt16)
            kk, qk = kq[:C], kq[C:]
            eye = jnp.where(row == col, kk, 0.0)
            rk_row = lax.rsqrt(jnp.sum(eye, axis=0, keepdims=True) + EPS)
            rk = lax.rsqrt(jnp.sum(k32 * k32, axis=1, keepdims=True) + EPS)
            rq = lax.rsqrt(jnp.sum(q32 * q32, axis=1, keepdims=True) + EPS) * (D**-0.5)
            kkn = kk * rk * rk_row
            qkn = qk * rq * rk_row
            g_rows = scal[kh, :, c * C : (c + 1) * C]
            cols = g_rows.T
            for e in range(2):
                g_row = g_rows[e : e + 1, :]
                g = cols[:, e : e + 1]
                b = cols[:, 2 + e : 3 + e]
                ratio = jnp.exp(jnp.where(row >= col, g - g_row, NEG))
                low = jnp.where(row > col, ratio * kkn * b, 0.0)
                eg = jnp.exp(g)
                g_end = g[C - 1 : C, :]
                v32 = vf[pl.ds(c * C * HEADS + 2 * kh + e, C, stride=HEADS), :]
                cells.append(dict(
                    low=low, sc=split(ratio * qkn), egq=eg * rq, e_end=jnp.exp(g_end),
                    out=jnp.exp(g_end - g) * rk,
                    rhs=jnp.concatenate([b * v32, (b * eg * rk) * k32], axis=1),
                ))
            qs.append((q32, q16))
            kts.append(kt16)
        invs = [-jnp.where((row >> 1) == (col >> 1), x["low"], 0.0) for x in cells]
        for lg in range(1, 7):
            here = ((row >> (lg + 1)) == (col >> (lg + 1))) & ((row >> lg) != (col >> lg))
            offs = [jnp.where(here, x["low"], 0.0) for x in cells]
            i16 = [x.astype(BF16) for x in invs]
            ys = [o + dot(i, o.astype(BF16)) for o, i in zip(offs, i16)]
            zs = [dot(y.astype(BF16), i) for y, i in zip(ys, i16)]
            invs = [v - (y + z) for v, y, z in zip(invs, ys, zs)]
        xs = [x["rhs"] + dot(i.astype(BF16), x["rhs"].astype(BF16)) for x, i in zip(cells, invs)]
        adds = []
        for c in range(NCH):
            kt2 = jnp.concatenate([kts[c], kts[c]], axis=1)
            for e in range(2):
                i = 2 * c + e
                h, l = split(cells[i]["out"] * xs[i])
                adds.append(dot(kt2, jnp.concatenate([h, l], axis=0)))
        rps, accs = [[None, None]], [[None, None]]
        for c in range(NCH):
            nrp, nacc = [], []
            for e in range(2):
                i = 2 * c + e
                e_end = cells[i]["e_end"]
                inc, neg = adds[i][:, :D], -adds[i][:, D:]
                if c == 0:
                    nrp.append(jnp.concatenate([inc, neg], axis=1))
                    nacc.append(e_end)
                else:
                    old, acc = rps[c][e], accs[c][e]
                    nrp.append(
                        e_end * old + jnp.concatenate([inc, acc * neg], axis=1)
                        + dot(neg.astype(BF16), old.astype(BF16))
                    )
                    nacc.append(e_end * acc)
            rps.append(nrp)
            accs.append(nacc)
        rp, acc = rps[NCH], accs[NCH]
        for e in range(2):
            hd = 2 * kh + e
            bh, bl = split(rp[e][:, :D])
            wire[hd, 0:C, 0:D] = rp[e][:, D:].astype(BF16)
            wire[hd, 0:C, D : 2 * D] = bh
            wire[hd, 0:C, 2 * D : 3 * D] = bl
            a = jnp.broadcast_to(acc[e], (16, 3 * D))
            a0 = a.astype(BF16).astype(F32)
            a1 = (a - a0).astype(BF16).astype(F32)
            a2 = a - a0 - a1
            lane = lax.broadcasted_iota(jnp.int32, (16, 3 * D), 1)
            wire[hd, C : C + 16, :] = jnp.where(
                lane < D, a0, jnp.where(lane < 2 * D, a1, a2)
            ).astype(BF16)

            @pl.when(hd == j)
            def _():
                maps[j] = wire[hd]

            @pl.when(hd != j)
            def _():
                map_copy(hd, j, zh * HALF + hd).start()
        for c in range(NCH):
            q32, q16 = qs[c]
            for e in range(2):
                hd = 2 * kh + e
                x = xs[2 * c + e]
                cell = cells[2 * c + e]
                if c == 0:
                    uw = jnp.concatenate([x[:, :D], -x[:, D:]], axis=1)
                else:
                    rp16 = rps[c][e].astype(BF16)
                    p = dot(x[:, D:].astype(BF16), rp16)
                    uw = jnp.concatenate(
                        [x[:, :D] - p[:, :D], -(accs[c][e] * x[:, D:] + p[:, D:])], axis=1
                    )
                uh, ul = split(uw)
                sch, scl = cell["sc"]
                og = dot(
                    jnp.concatenate([sch, scl, sch], axis=1),
                    jnp.concatenate([uh, uh, ul], axis=0),
                )
                direct = cell["egq"]
                if c > 0:
                    og = og + direct * dot(q16, rp16)
                    direct = direct * accs[c][e]
                o0[hd, c * C : (c + 1) * C, :] = og[:, :D]
                gh, gl = split(og[:, D:] + direct * q32)
                gq[hd, c * C : (c + 1) * C, :D] = gh
                gq[hd, c * C : (c + 1) * C, D:] = gl
        return 0

    lax.fori_loop(0, KHEADS, head, 0)
    for copy in loads[5:]:
        copy.wait()

    for s in range(HALF):
        @pl.when(s != j)
        def _():
            map_copy(0, s, w).wait_recv()

    first = jnp.where(zh == 0, 1.0, 0.0)
    ent[0] = jnp.concatenate([prior[...] * first, jnp.zeros((D, D), F32)], axis=1)
    mul[0] = jnp.ones((8, D), F32)

    def link(i, _):
        m16 = maps[i, 0:C, 0:D]
        add = maps[i, 0:C, D : 2 * D].astype(F32) + maps[i, 0:C, 2 * D : 3 * D].astype(F32)
        ar = maps[i, C : C + 16, :].astype(F32)
        a = (ar[0:8, 0:D] + ar[0:8, D : 2 * D]) + ar[0:8, 2 * D : 3 * D]
        x = ent[i]
        xh, xl = split(x[:, :D])
        mx = dot(m16, jnp.concatenate([xh, xl, x[:, D:].astype(BF16)], axis=1))
        acc = mul[i]
        a1 = a[0:1, :]
        r = a1 * x[:, :D] + (mx[:, :D] + mx[:, D : 2 * D]) + add
        p = a1 * x[:, D:] + mx[:, 2 * D :] + acc[0:1, :] * m16.astype(F32)
        ent[i + 1] = jnp.concatenate([r, p], axis=1)
        mul[i + 1] = a * acc
        return 0

    lax.fori_loop(0, HALF, link, 0)

    def z_copy(src, dst, i, to):
        return remote(src, dst, z_s.at[i], z_r.at[i], to)

    out_z[...] = ent[HALF].astype(BF16)
    to_one = [z_copy(out_z.at[:, pl.ds(0, D)], mid, 0, j + HALF)]
    to_zero = [
        z_copy(out_z, fin_z, 1, j),
        z_copy(mul.at[HALF], mul.at[HALF + 1], 2, j),
    ]

    def send_sin():
        for d in range(1, HALF):
            sin_copies[d - 1].start()

    sin_copies = [
        remote(
            sin16.at[(j + d) % HALF], sin.at[j], sin_s.at[d], sin_r.at[d],
            zh * HALF + (j + d) % HALF,
        )
        for d in range(1, HALF)
    ]
    fin_copies = [
        remote(finp, fin.at[j], fin_s.at[d], fin_r.at[d], zh * HALF + (j + d) % HALF)
        for d in range(1, HALF)
    ]

    @pl.when(zh == 0)
    def _():
        for copy in to_one:
            copy.start()

        def stage(i, _):
            sin16[i] = ent[i, :, 0:D].astype(BF16)
            return 0

        lax.fori_loop(0, HALF, stage, 0)
        send_sin()

    @pl.when(zh == 1)
    def _():
        for copy in to_zero:
            copy.start()

    for copy in att_copies:
        copy.wait()
    for i in range(4):
        own_k[2 * i : 2 * i + 2, :] = ak_ref[0, i].astype(F32)
    own = dot_nt(own_q[...], own_k[...].astype(BF16)) * (256**-0.5)
    r = lax.broadcasted_iota(jnp.int32, (16, 8), 0) // 4
    cc = lax.broadcasted_iota(jnp.int32, (16, 8), 1)
    own = jnp.where((cc % 2 == group) & (cc // 2 <= r), own, NEG)
    top = jnp.max(own, axis=1, keepdims=True)
    levels = []
    for s in range(WIDE):
        pk = parts[s, 16:32, :].astype(F32)
        lv = (pk[:, 0:1] + pk[:, 64:65]) + pk[:, 128:129]
        levels.append(lv)
        top = jnp.maximum(top, lv)
    pw = jnp.exp(own - top).astype(BF16)
    den = jnp.sum(pw.astype(F32), axis=1, keepdims=True)
    for i in range(4):
        own_k[2 * i : 2 * i + 2, :] = av_ref[0, i].astype(F32)
    num = dot(pw, own_k[...].astype(BF16))
    for s in range(WIDE):
        wt = jnp.exp(levels[s] - top)
        den = den + wt
        num = num + wt * parts[s, 0:16, :].astype(F32)
    for i in range(4):
        a0s[4 * i : 4 * i + 4, :] = ag_ref[0, i].astype(F32)
    done = num / den * sigmoid(a0s[...])
    for half in range(2):
        a1s[...] = done[:, half * 128 : (half + 1) * 128]
        for h in range(4):
            at = h * 256 + half * 128
            att_ref[0, :, at : at + 128] = a1s[pl.ds(h, 4, stride=4), :].astype(BF16)

    gain = gain_ref[...]
    vf[...] = gv[...].astype(F32)

    def gates(h, _):
        z = vf[pl.ds(h, TOK, stride=HEADS), :]
        cf[pl.ds(pl.multiple_of(h * TOK, TOK), TOK), :] = z * sigmoid(z) * gain
        return 0

    lax.fori_loop(0, HEADS, gates, 0)

    @pl.when(zh == 1)
    def _():
        to_one[0].wait_recv()
        s16 = mid[...]
        s32 = s16.astype(F32)

        def enter(i):
            x = ent[i]
            y = dot(x[:, D:].astype(BF16), s16)
            return (x[:, :D] + mul[i, 0:1, :] * s32 + y).astype(BF16)

        for d in range(1, HALF):
            to = (j + d) % HALF
            sin16[to] = enter(to)
            sin_copies[d - 1].start()
        finp[...] = enter(HALF)
        sin16[j] = enter(j)

    @pl.when(zh == 0)
    def _():
        for copy in to_zero:
            copy.wait_recv()
        s = ent[HALF, :, 0:D]
        sh, sl = split(s)
        x = fin_z[...]
        y = dot(x[:, D:], jnp.concatenate([sh, sl], axis=1))
        finp[...] = (
            x[:, :D].astype(F32) + mul[HALF + 1, 0:1, :] * s + (y[:, :D] + y[:, D:])
        ).astype(BF16)

    for copy in fin_copies:
        copy.start()
    fin[j] = finp[...]
    sin[j] = sin16[j]
    for d in range(HALF):
        h = (j + HALF - d) % HALF
        if d > 0:
            sin_copies[d - 1].wait_recv()
        s = sin[h]
        o = o0[h] + dot(gq[h], jnp.concatenate([s, s], axis=0))
        scale = lax.rsqrt(jnp.mean(o * o, axis=1, keepdims=True) + EPS)
        z = cf[pl.ds(pl.multiple_of(h * TOK, TOK), TOK), :]
        out_ref[:, pl.ds(pl.multiple_of(h * D, D), D)] = (o * scale * z).astype(BF16)

    kraw, qraw = [], []
    for i in range(4):
        for ref, at, keep in ((sk_ref, 0, kraw), (sq_ref, 4, qraw)):
            x = ref[0, i].astype(F32)
            kqs[pl.ds(at + i, KHEADS, stride=8), :] = x
            uscr[pl.ds(0, KHEADS, stride=2), :] = x
            uscr[pl.ds(1, KHEADS, stride=2), :] = x
            keep.append(uscr[0:HEADS, :])
    rk = [lax.rsqrt(jnp.sum(x * x, axis=1, keepdims=True) + EPS) for x in kraw]
    rq = [lax.rsqrt(jnp.sum(x * x, axis=1, keepdims=True) + EPS) * (D**-0.5) for x in qraw]
    kn = [x * r for x, r in zip(kraw, rk)]
    qn = [x * r for x, r in zip(qraw, rq)]
    diag = lax.broadcasted_iota(jnp.int32, (HEADS, HEADS), 0) == lax.broadcasted_iota(
        jnp.int32, (HEADS, HEADS), 1
    )

    def column(x):
        return jnp.sum(jnp.where(diag, x, 0.0), axis=1, keepdims=True)

    sb = sigmoid(sb_ref[0])
    sd = sd_ref[0]
    beta = [column(sb[i : i + 1, :]) for i in range(4)]
    cum = [column(sd[0:1, :])]
    for i in range(1, 4):
        cum.append(cum[-1] + column(sd[i : i + 1, :]))
    for copy in fin_copies:
        copy.wait()
    for h in range(HEADS):
        kh = h // 2
        res[h * 8 : (h + 1) * 8, :] = dot(kqs[kh * 8 : (kh + 1) * 8, :].astype(BF16), fin[h])
    us = []
    for i in range(4):
        ks = res[pl.ds(i, HEADS, stride=8), :] * (rk[i] * jnp.exp(cum[i]))
        u = sv_ref[0, i].astype(F32) - ks
        for p in range(i):
            kk = jnp.sum(kn[i] * kn[p], axis=1, keepdims=True)
            u = u - (jnp.exp(cum[i] - cum[p]) * kk) * us[p]
        u = beta[i] * u
        us.append(u)
        o = res[pl.ds(4 + i, HEADS, stride=8), :] * (rq[i] * jnp.exp(cum[i]))
        for p in range(i + 1):
            qk = jnp.sum(qn[i] * kn[p], axis=1, keepdims=True)
            o = o + (jnp.exp(cum[i] - cum[p]) * qk) * us[p]
        scale = lax.rsqrt(jnp.mean(o * o, axis=1, keepdims=True) + EPS)
        z = sg_ref[0, i].astype(F32)
        sscr[i * 8 : (i + 1) * 8, :] = o * scale * gain * (z * sigmoid(z))
    for h in range(HEADS):
        step_ref[0, :, h * D : (h + 1) * D] = sscr[pl.ds(h, 4, stride=8), :].astype(BF16)
    for i in range(4):
        uscr[pl.ds(i, HEADS, stride=8), :] = us[i] * (jnp.exp(cum[3] - cum[i]) * rk[i])
        uscr[pl.ds(4 + i, HEADS, stride=8), :] = jnp.zeros((HEADS, D), F32)
    decay = jnp.broadcast_to(jnp.exp(cum[3]), (HEADS, D))
    for h in range(HEADS):
        kh = h // 2
        uh, ul = split(uscr[h * 8 : (h + 1) * 8, :])
        y = dot_tn(
            kqs[kh * 8 : (kh + 1) * 8, :].astype(BF16), jnp.concatenate([uh, ul], axis=1)
        )
        state_ref[0, h] = decay[h : h + 1, :] * fin[h].astype(F32) + (y[:, :D] + y[:, D:])

    for hd in range(HALF):
        @pl.when(hd != j)
        def _():
            map_copy(hd, 0, w).wait_send()

    for copy in sin_copies:
        copy.wait_send()

    @pl.when(zh == 0)
    def _():
        to_one[0].wait_send()

    @pl.when(zh == 1)
    def _():
        for copy in to_zero:
            copy.wait_send()


def hand_out(a, b, c, d, ao, bo, co, do):
    for src, dst in ((a, ao), (b, bo), (c, co), (d, do)):
        dst[...] = src[...]


def shards(
    span_query, span_key, span_value, span_beta_logit, span_logdecay, span_gate,
    norm_gain, prior_state,
    step_query, step_key, step_value, step_beta_logit, step_logdecay, step_gate,
    cache_key, cache_value, att_query, att_key, att_value, att_gate,
):
    def rows(c):
        return c.reshape(2048, 2, 2, 128).transpose(0, 2, 1, 3).reshape(8192, 128)

    vm = pl.BlockSpec(memory_space=pltpu.VMEM)
    hbm = pl.BlockSpec(memory_space=pltpu.HBM)
    sem = pltpu.SemaphoreType.DMA
    V = pltpu.VMEM
    results = pl.pallas_call(
        kernel,
        out_shape=(
            V((TOK, HEADS * D), BF16),
            V((1, 4, HEADS * D), BF16),
            V((1, HEADS, D, D), F32),
            V((1, 4, 1024), BF16),
        ),
        in_specs=[hbm, hbm, hbm, vm, vm, hbm, vm, hbm] + [vm] * 6 + [hbm, hbm] + [vm] * 4,
        out_specs=(vm,) * 4,
        scratch_shapes=[
            V((TOK * KHEADS, D), BF16), V((TOK * KHEADS, D), BF16), V((TOK * HEADS, D), BF16),
            V((TOK * HEADS, D), BF16), V((8192, D), BF16), V((8192, D), BF16), V((D, D), F32),
            V((TOK * KHEADS, D), F32), V((TOK * KHEADS, D), F32), V((TOK * HEADS, D), F32),
            V((8192, D), F32), V((2048, 256), BF16), V((2048, 256), BF16), V((256, 2048), F32),
            V((KHEADS, 8, TOK), F32),
            V((HEADS, C + 16, 3 * D), BF16), V((HALF, C + 16, 3 * D), BF16),
            V((HEADS, TOK, D), F32), V((HEADS, TOK, 2 * D), BF16),
            V((HALF + 1, D, 2 * D), F32), V((HALF + 2, 8, D), F32), V((D, D), BF16),
            V((D, 2 * D), BF16), V((D, 2 * D), BF16),
            V((HALF + 1, D, D), BF16), V((HALF, D, D), BF16), V((D, D), BF16),
            V((HALF, D, D), BF16),
            V((16, 256), BF16), V((WIDE, 16, 256), BF16),
            V((WIDE, 32, 256), BF16), V((WIDE, 32, 256), BF16),
            V((32, D), F32), V((64, D), F32), V((64, D), F32), V((32, D), F32),
            V((16, 256), F32), V((16, D), F32), V((8, 256), F32),
            sem((8,)), sem((WIDE,)), sem((WIDE,)), sem((WIDE,)), sem((WIDE,)),
            sem((HALF,)), sem((HALF,)), sem((HALF,)), sem((HALF,)), sem((HALF,)), sem((HALF,)),
            sem((3,)), sem((3,)),
        ],
        compiler_params=pltpu.CompilerParams(
            collective_id=0, has_side_effects=True, vmem_limit_bytes=58 * 2**20
        ),
        name="rollout_fork",
    )(
        span_query.reshape(TOK * KHEADS, D), span_key.reshape(TOK * KHEADS, D),
        span_value.reshape(TOK * HEADS, D), span_beta_logit.T, span_logdecay.T,
        span_gate.reshape(TOK * HEADS, D), norm_gain.reshape(1, D), prior_state,
        step_query, step_key, step_value, step_beta_logit, step_logdecay, step_gate,
        rows(cache_key), rows(cache_value), att_query, att_key, att_value, att_gate,
    )
    return pl.pallas_call(
        hand_out,
        out_shape=tuple(jax.ShapeDtypeStruct(x.shape, x.dtype) for x in results),
        in_specs=[vm] * 4,
        out_specs=(vm,) * 4,
        compiler_params=pltpu.CompilerParams(vmem_limit_bytes=8 * 2**20),
        name="hand_out",
    )(*results)


def solution(mesh):
    tok = P(("prompt", "wide"), "tp", None)
    tok2 = P(("prompt", "wide"), "tp")
    stp = P(("prompt", "wide"), None, "tp", None)
    stp2 = P(("prompt", "wide"), None, "tp")
    in_specs = (
        tok, tok, tok, tok2, tok2, tok, P(), P(("prompt", "tp"), None, None),
        stp, stp, stp, stp2, stp2, stp,
        P(("prompt", "wide"), None, None), P(("prompt", "wide"), None, None),
        stp, P(("prompt", "wide"), None, None, None), P(("prompt", "wide"), None, None, None), stp,
    )
    out_specs = (
        P(("prompt", "wide"), "tp"),
        stp2,
        P(("prompt", "wide"), "tp", None, None),
        stp2,
    )
    return jax.shard_map(shards, mesh=mesh, in_specs=in_specs, out_specs=out_specs, check_vma=False)
```

```python
import jax
import jax.numpy as jnp
from jax import lax
from jax.experimental import pallas as pl
from jax.experimental.pallas import tpu as pltpu
from jax.sharding import PartitionSpec as P

F32 = jnp.float32
BF16 = jnp.bfloat16
MESH = pl.DeviceIdType.MESH
EPS = 1e-6
C = 128
D = 128
HEADS = 8
KHEADS = 4
TOK = 512
NCH = TOK // C
HALF = 8
WIDE = 16
NEG = -1e30


def dot(a, b):
    return lax.dot_general(a, b, (((1,), (0,)), ((), ())), preferred_element_type=F32)


def dot_nt(a, b):
    return lax.dot_general(a, b, (((1,), (1,)), ((), ())), preferred_element_type=F32)


def dot_tn(a, b):
    return lax.dot_general(a, b, (((0,), (0,)), ((), ())), preferred_element_type=F32)


def split(x):
    hi = x.astype(BF16)
    return hi, (x - hi.astype(F32)).astype(BF16)


def sigmoid(x):
    return 1.0 / (1.0 + jnp.exp(-x))


def kernel(
    q_hbm, k_hbm, v_hbm, bl_ref, ld_ref, gate_hbm, gain_ref, prior_hbm,
    sq_ref, sk_ref, sv_ref, sb_ref, sd_ref, sg_ref,
    ck_hbm, cv_hbm, aq_ref, ak_ref, av_ref, ag_ref,
    out_ref, step_ref, state_ref, att_ref,
    qv, kv, vv, gv, ckv, cvv, prior,
    qf, kf, vf, cf, kc, vc, scores, scal,
    wire, maps, o0, gq, ent, mul, mid, fin_z, out_z,
    sin16, sin, finp, fin, own_q, all_q, msg, parts,
    kqs, res, uscr, sscr, a0s, a1s, own_k,
    load, q_s, q_r, att_s, att_r, map_s, map_r, sin_s, sin_r, fin_s, fin_r, z_s, z_r,
):
    w = lax.axis_index("wide")
    zh = w // HALF
    j = w % HALF
    group = lax.axis_index("tp") // 2

    loads = []
    for i, (src, dst) in enumerate((
        (q_hbm, qv), (k_hbm, kv), (v_hbm, vv), (ck_hbm, ckv), (cv_hbm, cvv), (gate_hbm, gv),
        (prior_hbm.at[j], prior),
    )):
        copy = pltpu.make_async_copy(src, dst, load.at[i])
        copy.start()
        loads.append(copy)

    barrier = pltpu.get_barrier_semaphore()
    for d in range(1, WIDE):
        pl.semaphore_signal(
            barrier, inc=1, device_id={"wide": (w + d) % WIDE}, device_id_type=MESH
        )
    for i in range(4):
        a0s[4 * i : 4 * i + 4, :] = aq_ref[0, i].astype(F32)
    own_q[...] = a0s[...].astype(BF16)
    upper = (
        lax.broadcasted_iota(jnp.int32, (C, C), 0) <= lax.broadcasted_iota(jnp.int32, (C, C), 1)
    ).astype(F32)
    scal[...] = jnp.zeros_like(scal)
    for c in range(NCH):
        part = slice(c * C, (c + 1) * C)
        g8 = lax.dot_general(
            ld_ref[:, part], upper, (((1,), (0,)), ((), ())),
            precision=lax.Precision.HIGHEST, preferred_element_type=F32,
        )
        b8 = sigmoid(bl_ref[:, part])
        for kh in range(KHEADS):
            scal[kh, 0:2, part] = g8[2 * kh : 2 * kh + 2]
            scal[kh, 2:4, part] = b8[2 * kh : 2 * kh + 2]

    for copy in loads[:3]:
        copy.wait()
    qf[...] = qv[...].astype(F32)
    kf[...] = kv[...].astype(F32)
    vf[...] = vv[...].astype(F32)
    pl.semaphore_wait(barrier, WIDE - 1)

    def remote(src, dst, ss, rs, to):
        return pltpu.make_async_remote_copy(
            src_ref=src, dst_ref=dst, send_sem=ss, recv_sem=rs,
            device_id={"wide": to}, device_id_type=MESH,
        )

    def map_copy(to, slot, device):
        return remote(wire.at[to], maps.at[slot], map_s.at[to], map_r.at[slot], device)

    q_copies = []
    for d in range(1, WIDE):
        copy = remote(own_q, all_q.at[w], q_s.at[d], q_r.at[d], (w + d) % WIDE)
        copy.start()
        q_copies.append(copy)
    all_q[w] = own_q[...]

    att_copies = []
    for d in range(1, WIDE):
        to = (w + d) % WIDE
        att_copies.append(remote(msg.at[to], parts.at[w], att_s.at[d], att_r.at[d], to))

    def attend():
        for load_copy, raw, cut in ((loads[3], ckv, kc), (loads[4], cvv, vc)):
            load_copy.wait()
            cf[...] = raw[...].astype(F32)
            cut[:, 0:128] = cf[pl.ds(group, 2048, stride=4), :].astype(BF16)
            cut[:, 128:256] = cf[pl.ds(2 + group, 2048, stride=4), :].astype(BF16)
        for copy in q_copies:
            copy.wait()
        scores[...] = dot_nt(all_q[...].reshape(256, 256), kc[...]) * (256**-0.5)
        sc = scores[...]
        top = jnp.max(sc, axis=1, keepdims=True)
        wt = jnp.exp(sc - top).astype(BF16)
        total = jnp.sum(wt.astype(F32), axis=1, keepdims=True)
        num = (dot(wt, vc[...]) / total).astype(BF16)
        level = top + jnp.log(total)
        l0 = level.astype(BF16).astype(F32)
        l1 = (level - l0).astype(BF16).astype(F32)
        l2 = level - l0 - l1
        lane = lax.broadcasted_iota(jnp.int32, (256, 256), 1)
        packed = jnp.where(lane < 64, l0, jnp.where(lane < 128, l1, l2)).astype(BF16)
        for s in range(WIDE):
            msg[s, 0:16, :] = num[s * 16 : (s + 1) * 16, :]
            msg[s, 16:32, :] = packed[s * 16 : (s + 1) * 16, :]
        for copy in att_copies:
            copy.start()
        parts[w] = msg[w]

    row = lax.broadcasted_iota(jnp.int32, (C, C), 0)
    col = lax.broadcasted_iota(jnp.int32, (C, C), 1)

    def head(it, _):
        kh = (j // 2 + jnp.where(it == 0, 2, 0) + jnp.where(it == 1, 1, 0)
              + jnp.where(it == 2, 3, 0)) % KHEADS

        @pl.when(it == 2)
        def _():
            attend()

        ks, qs, kts, cells = [], [], [], []
        for c in range(NCH):
            k32 = kf[pl.ds(c * C * KHEADS + kh, C, stride=KHEADS), :]
            q32 = qf[pl.ds(c * C * KHEADS + kh, C, stride=KHEADS), :]
            k16 = k32.astype(BF16)
            q16 = q32.astype(BF16)
            kt16 = k32.T.astype(BF16)
            kq = dot_nt(jnp.concatenate([k16, q16], axis=0), k16)
            kk, qk = kq[:C], kq[C:]
            eye = jnp.where(row == col, kk, 0.0)
            rk_row = lax.rsqrt(jnp.sum(eye, axis=0, keepdims=True) + EPS)
            rk = lax.rsqrt(jnp.sum(k32 * k32, axis=1, keepdims=True) + EPS)
            rq = lax.rsqrt(jnp.sum(q32 * q32, axis=1, keepdims=True) + EPS) * (D**-0.5)
            kkn = kk * rk * rk_row
            qkn = qk * rq * rk_row
            g_rows = scal[kh, :, c * C : (c + 1) * C]
            cols = g_rows.T
            for e in range(2):
                g_row = g_rows[e : e + 1, :]
                g = cols[:, e : e + 1]
                b = cols[:, 2 + e : 3 + e]
                ratio = jnp.exp(jnp.where(row >= col, g - g_row, NEG))
                low = jnp.where(row > col, ratio * kkn * b, 0.0)
                eg = jnp.exp(g)
                g_end = g[C - 1 : C, :]
                v32 = vf[pl.ds(c * C * HEADS + 2 * kh + e, C, stride=HEADS), :]
                cells.append(dict(
                    low=low, sc=split(ratio * qkn), egq=eg * rq, e_end=jnp.exp(g_end),
                    out=jnp.exp(g_end - g) * rk,
                    rhs=jnp.concatenate([b * v32, (b * eg * rk) * k32], axis=1),
                ))
            qs.append((q32, q16))
            kts.append(kt16)
        near = (row >> 2) == (col >> 2)
        lows = [jnp.where(near, x["low"], 0.0) for x in cells]
        l16 = [x.astype(BF16) for x in lows]
        sq = [dot(x, x) for x in l16]
        cu = [dot(x.astype(BF16), y) for x, y in zip(sq, l16)]
        invs = [x - y - z for x, y, z in zip(sq, lows, cu)]
        for lg in range(2, 7):
            here = ((row >> (lg + 1)) == (col >> (lg + 1))) & ((row >> lg) != (col >> lg))
            offs = [jnp.where(here, x["low"], 0.0) for x in cells]
            i16 = [x.astype(BF16) for x in invs]
            ys = [o + dot(i, o.astype(BF16)) for o, i in zip(offs, i16)]
            zs = [dot(y.astype(BF16), i) for y, i in zip(ys, i16)]
            invs = [v - (y + z) for v, y, z in zip(invs, ys, zs)]
        xs = [x["rhs"] + dot(i.astype(BF16), x["rhs"].astype(BF16)) for x, i in zip(cells, invs)]
        adds = []
        for c in range(NCH):
            kt2 = jnp.concatenate([kts[c], kts[c]], axis=1)
            for e in range(2):
                i = 2 * c + e
                h, l = split(cells[i]["out"] * xs[i])
                adds.append(dot(kt2, jnp.concatenate([h, l], axis=0)))
        rps, accs = [[None, None]], [[None, None]]
        for c in range(NCH):
            nrp, nacc = [], []
            for e in range(2):
                i = 2 * c + e
                e_end = cells[i]["e_end"]
                inc, neg = adds[i][:, :D], -adds[i][:, D:]
                if c == 0:
                    nrp.append(jnp.concatenate([inc, neg], axis=1))
                    nacc.append(e_end)
                else:
                    old, acc = rps[c][e], accs[c][e]
                    nrp.append(
                        e_end * old + jnp.concatenate([inc, acc * neg], axis=1)
                        + dot(neg.astype(BF16), old.astype(BF16))
                    )
                    nacc.append(e_end * acc)
            rps.append(nrp)
            accs.append(nacc)
        rp, acc = rps[NCH], accs[NCH]
        for e in range(2):
            hd = 2 * kh + e
            bh, bl = split(rp[e][:, :D])
            wire[hd, 0:C, 0:D] = rp[e][:, D:].astype(BF16)
            wire[hd, 0:C, D : 2 * D] = bh
            wire[hd, 0:C, 2 * D : 3 * D] = bl
            a = jnp.broadcast_to(acc[e], (16, 3 * D))
            a0 = a.astype(BF16).astype(F32)
            a1 = (a - a0).astype(BF16).astype(F32)
            a2 = a - a0 - a1
            lane = lax.broadcasted_iota(jnp.int32, (16, 3 * D), 1)
            wire[hd, C : C + 16, :] = jnp.where(
                lane < D, a0, jnp.where(lane < 2 * D, a1, a2)
            ).astype(BF16)

            @pl.when(hd == j)
            def _():
                maps[j] = wire[hd]

            @pl.when(hd != j)
            def _():
                map_copy(hd, j, zh * HALF + hd).start()
        for c in range(NCH):
            q32, q16 = qs[c]
            for e in range(2):
                hd = 2 * kh + e
                x = xs[2 * c + e]
                cell = cells[2 * c + e]
                if c == 0:
                    uw = jnp.concatenate([x[:, :D], -x[:, D:]], axis=1)
                else:
                    rp16 = rps[c][e].astype(BF16)
                    p = dot(x[:, D:].astype(BF16), rp16)
                    uw = jnp.concatenate(
                        [x[:, :D] - p[:, :D], -(accs[c][e] * x[:, D:] + p[:, D:])], axis=1
                    )
                uh, ul = split(uw)
                sch, scl = cell["sc"]
                og = dot(
                    jnp.concatenate([sch, scl, sch], axis=1),
                    jnp.concatenate([uh, uh, ul], axis=0),
                )
                direct = cell["egq"]
                if c > 0:
                    og = og + direct * dot(q16, rp16)
                    direct = direct * accs[c][e]
                o0[hd, c * C : (c + 1) * C, :] = og[:, :D]
                gh, gl = split(og[:, D:] + direct * q32)
                gq[hd, c * C : (c + 1) * C, :D] = gh
                gq[hd, c * C : (c + 1) * C, D:] = gl
        return 0

    lax.fori_loop(0, KHEADS, head, 0)
    for copy in loads[5:]:
        copy.wait()

    for s in range(HALF):
        @pl.when(s != j)
        def _():
            map_copy(0, s, w).wait_recv()

    first = jnp.where(zh == 0, 1.0, 0.0)
    ent[0] = jnp.concatenate([prior[...] * first, jnp.zeros((D, D), F32)], axis=1)
    mul[0] = jnp.ones((8, D), F32)

    def link(i, _):
        m16 = maps[i, 0:C, 0:D]
        add = maps[i, 0:C, D : 2 * D].astype(F32) + maps[i, 0:C, 2 * D : 3 * D].astype(F32)
        ar = maps[i, C : C + 16, :].astype(F32)
        a = (ar[0:8, 0:D] + ar[0:8, D : 2 * D]) + ar[0:8, 2 * D : 3 * D]
        x = ent[i]
        xh, xl = split(x[:, :D])
        mx = dot(m16, jnp.concatenate([xh, xl, x[:, D:].astype(BF16)], axis=1))
        acc = mul[i]
        a1 = a[0:1, :]
        r = a1 * x[:, :D] + (mx[:, :D] + mx[:, D : 2 * D]) + add
        p = a1 * x[:, D:] + mx[:, 2 * D :] + acc[0:1, :] * m16.astype(F32)
        ent[i + 1] = jnp.concatenate([r, p], axis=1)
        mul[i + 1] = a * acc
        return 0

    lax.fori_loop(0, HALF, link, 0)

    def z_copy(src, dst, i, to):
        return remote(src, dst, z_s.at[i], z_r.at[i], to)

    out_z[...] = ent[HALF].astype(BF16)
    to_one = [z_copy(out_z.at[:, pl.ds(0, D)], mid, 0, j + HALF)]
    to_zero = [
        z_copy(out_z, fin_z, 1, j),
        z_copy(mul.at[HALF], mul.at[HALF + 1], 2, j),
    ]

    def send_sin():
        for d in range(1, HALF):
            sin_copies[d - 1].start()

    sin_copies = [
        remote(
            sin16.at[(j + d) % HALF], sin.at[j], sin_s.at[d], sin_r.at[d],
            zh * HALF + (j + d) % HALF,
        )
        for d in range(1, HALF)
    ]
    fin_copies = [
        remote(finp, fin.at[j], fin_s.at[d], fin_r.at[d], zh * HALF + (j + d) % HALF)
        for d in range(1, HALF)
    ]

    @pl.when(zh == 0)
    def _():
        for copy in to_one:
            copy.start()

        def stage(i, _):
            sin16[i] = ent[i, :, 0:D].astype(BF16)
            return 0

        lax.fori_loop(0, HALF, stage, 0)
        send_sin()

    @pl.when(zh == 1)
    def _():
        for copy in to_zero:
            copy.start()

    for copy in att_copies:
        copy.wait()
    for i in range(4):
        own_k[2 * i : 2 * i + 2, :] = ak_ref[0, i].astype(F32)
    own = dot_nt(own_q[...], own_k[...].astype(BF16)) * (256**-0.5)
    r = lax.broadcasted_iota(jnp.int32, (16, 8), 0) // 4
    cc = lax.broadcasted_iota(jnp.int32, (16, 8), 1)
    own = jnp.where((cc % 2 == group) & (cc // 2 <= r), own, NEG)
    top = jnp.max(own, axis=1, keepdims=True)
    levels = []
    for s in range(WIDE):
        pk = parts[s, 16:32, :].astype(F32)
        lv = (pk[:, 0:1] + pk[:, 64:65]) + pk[:, 128:129]
        levels.append(lv)
        top = jnp.maximum(top, lv)
    pw = jnp.exp(own - top).astype(BF16)
    den = jnp.sum(pw.astype(F32), axis=1, keepdims=True)
    for i in range(4):
        own_k[2 * i : 2 * i + 2, :] = av_ref[0, i].astype(F32)
    num = dot(pw, own_k[...].astype(BF16))
    for s in range(WIDE):
        wt = jnp.exp(levels[s] - top)
        den = den + wt
        num = num + wt * parts[s, 0:16, :].astype(F32)
    for i in range(4):
        a0s[4 * i : 4 * i + 4, :] = ag_ref[0, i].astype(F32)
    done = num / den * sigmoid(a0s[...])
    for half in range(2):
        a1s[...] = done[:, half * 128 : (half + 1) * 128]
        for h in range(4):
            at = h * 256 + half * 128
            att_ref[0, :, at : at + 128] = a1s[pl.ds(h, 4, stride=4), :].astype(BF16)

    gain = gain_ref[...]
    vf[...] = gv[...].astype(F32)

    def gates(h, _):
        z = vf[pl.ds(h, TOK, stride=HEADS), :]
        cf[pl.ds(pl.multiple_of(h * TOK, TOK), TOK), :] = z * sigmoid(z) * gain
        return 0

    lax.fori_loop(0, HEADS, gates, 0)

    kraw, qraw = [], []
    for i in range(4):
        for ref, at, keep in ((sk_ref, 0, kraw), (sq_ref, 4, qraw)):
            x = ref[0, i].astype(F32)
            kqs[pl.ds(at + i, KHEADS, stride=8), :] = x
            uscr[pl.ds(0, KHEADS, stride=2), :] = x
            uscr[pl.ds(1, KHEADS, stride=2), :] = x
            keep.append(uscr[0:HEADS, :])
    rk = [lax.rsqrt(jnp.sum(x * x, axis=1, keepdims=True) + EPS) for x in kraw]
    rq = [lax.rsqrt(jnp.sum(x * x, axis=1, keepdims=True) + EPS) * (D**-0.5) for x in qraw]
    kn = [x * r for x, r in zip(kraw, rk)]
    qn = [x * r for x, r in zip(qraw, rq)]
    diag = lax.broadcasted_iota(jnp.int32, (HEADS, HEADS), 0) == lax.broadcasted_iota(
        jnp.int32, (HEADS, HEADS), 1
    )

    def column(x):
        return jnp.sum(jnp.where(diag, x, 0.0), axis=1, keepdims=True)

    sb = sigmoid(sb_ref[0])
    sd = sd_ref[0]
    beta = [column(sb[i : i + 1, :]) for i in range(4)]
    cum = [column(sd[0:1, :])]
    for i in range(1, 4):
        cum.append(cum[-1] + column(sd[i : i + 1, :]))

    @pl.when(zh == 1)
    def _():
        to_one[0].wait_recv()
        s16 = mid[...]
        s32 = s16.astype(F32)

        def enter(i):
            x = ent[i]
            y = dot(x[:, D:].astype(BF16), s16)
            return (x[:, :D] + mul[i, 0:1, :] * s32 + y).astype(BF16)

        for d in range(1, HALF):
            to = (j + d) % HALF
            sin16[to] = enter(to)
            sin_copies[d - 1].start()
        finp[...] = enter(HALF)
        for copy in fin_copies:
            copy.start()
        sin16[j] = enter(j)

    @pl.when(zh == 0)
    def _():
        for copy in to_zero:
            copy.wait_recv()
        s = ent[HALF, :, 0:D]
        sh, sl = split(s)
        x = fin_z[...]
        y = dot(x[:, D:], jnp.concatenate([sh, sl], axis=1))
        finp[...] = (
            x[:, :D].astype(F32) + mul[HALF + 1, 0:1, :] * s + (y[:, :D] + y[:, D:])
        ).astype(BF16)

        for copy in fin_copies:
            copy.start()

    fin[j] = finp[...]
    sin[j] = sin16[j]
    for d in range(HALF):
        h = (j + HALF - d) % HALF
        if d > 0:
            sin_copies[d - 1].wait_recv()
        s = sin[h]
        o = o0[h] + dot(gq[h], jnp.concatenate([s, s], axis=0))
        scale = lax.rsqrt(jnp.mean(o * o, axis=1, keepdims=True) + EPS)
        z = cf[pl.ds(pl.multiple_of(h * TOK, TOK), TOK), :]
        out_ref[:, pl.ds(pl.multiple_of(h * D, D), D)] = (o * scale * z).astype(BF16)

    for copy in fin_copies:
        copy.wait()
    for h in range(HEADS):
        kh = h // 2
        res[h * 8 : (h + 1) * 8, :] = dot(kqs[kh * 8 : (kh + 1) * 8, :].astype(BF16), fin[h])
    us = []
    for i in range(4):
        ks = res[pl.ds(i, HEADS, stride=8), :] * (rk[i] * jnp.exp(cum[i]))
        u = sv_ref[0, i].astype(F32) - ks
        for p in range(i):
            kk = jnp.sum(kn[i] * kn[p], axis=1, keepdims=True)
            u = u - (jnp.exp(cum[i] - cum[p]) * kk) * us[p]
        u = beta[i] * u
        us.append(u)
        o = res[pl.ds(4 + i, HEADS, stride=8), :] * (rq[i] * jnp.exp(cum[i]))
        for p in range(i + 1):
            qk = jnp.sum(qn[i] * kn[p], axis=1, keepdims=True)
            o = o + (jnp.exp(cum[i] - cum[p]) * qk) * us[p]
        scale = lax.rsqrt(jnp.mean(o * o, axis=1, keepdims=True) + EPS)
        z = sg_ref[0, i].astype(F32)
        sscr[i * 8 : (i + 1) * 8, :] = o * scale * gain * (z * sigmoid(z))
    for h in range(HEADS):
        step_ref[0, :, h * D : (h + 1) * D] = sscr[pl.ds(h, 4, stride=8), :].astype(BF16)
    for i in range(4):
        uscr[pl.ds(i, HEADS, stride=8), :] = us[i] * (jnp.exp(cum[3] - cum[i]) * rk[i])
        uscr[pl.ds(4 + i, HEADS, stride=8), :] = jnp.zeros((HEADS, D), F32)
    decay = jnp.broadcast_to(jnp.exp(cum[3]), (HEADS, D))
    for h in range(HEADS):
        kh = h // 2
        uh, ul = split(uscr[h * 8 : (h + 1) * 8, :])
        y = dot_tn(
            kqs[kh * 8 : (kh + 1) * 8, :].astype(BF16), jnp.concatenate([uh, ul], axis=1)
        )
        state_ref[0, h] = decay[h : h + 1, :] * fin[h].astype(F32) + (y[:, :D] + y[:, D:])

    for hd in range(HALF):
        @pl.when(hd != j)
        def _():
            map_copy(hd, 0, w).wait_send()

    for copy in sin_copies:
        copy.wait_send()

    @pl.when(zh == 0)
    def _():
        to_one[0].wait_send()

    @pl.when(zh == 1)
    def _():
        for copy in to_zero:
            copy.wait_send()


def hand_out(a, b, c, d, ao, bo, co, do):
    for src, dst in ((a, ao), (b, bo), (c, co), (d, do)):
        dst[...] = src[...]


def shards(
    span_query, span_key, span_value, span_beta_logit, span_logdecay, span_gate,
    norm_gain, prior_state,
    step_query, step_key, step_value, step_beta_logit, step_logdecay, step_gate,
    cache_key, cache_value, att_query, att_key, att_value, att_gate,
):
    def rows(c):
        return c.reshape(2048, 2, 2, 128).transpose(0, 2, 1, 3).reshape(8192, 128)

    vm = pl.BlockSpec(memory_space=pltpu.VMEM)
    hbm = pl.BlockSpec(memory_space=pltpu.HBM)
    sem = pltpu.SemaphoreType.DMA
    V = pltpu.VMEM
    results = pl.pallas_call(
        kernel,
        out_shape=(
            V((TOK, HEADS * D), BF16),
            V((1, 4, HEADS * D), BF16),
            V((1, HEADS, D, D), F32),
            V((1, 4, 1024), BF16),
        ),
        in_specs=[hbm, hbm, hbm, vm, vm, hbm, vm, hbm] + [vm] * 6 + [hbm, hbm] + [vm] * 4,
        out_specs=(vm,) * 4,
        scratch_shapes=[
            V((TOK * KHEADS, D), BF16), V((TOK * KHEADS, D), BF16), V((TOK * HEADS, D), BF16),
            V((TOK * HEADS, D), BF16), V((8192, D), BF16), V((8192, D), BF16), V((D, D), F32),
            V((TOK * KHEADS, D), F32), V((TOK * KHEADS, D), F32), V((TOK * HEADS, D), F32),
            V((8192, D), F32), V((2048, 256), BF16), V((2048, 256), BF16), V((256, 2048), F32),
            V((KHEADS, 8, TOK), F32),
            V((HEADS, C + 16, 3 * D), BF16), V((HALF, C + 16, 3 * D), BF16),
            V((HEADS, TOK, D), F32), V((HEADS, TOK, 2 * D), BF16),
            V((HALF + 1, D, 2 * D), F32), V((HALF + 2, 8, D), F32), V((D, D), BF16),
            V((D, 2 * D), BF16), V((D, 2 * D), BF16),
            V((HALF + 1, D, D), BF16), V((HALF, D, D), BF16), V((D, D), BF16),
            V((HALF, D, D), BF16),
            V((16, 256), BF16), V((WIDE, 16, 256), BF16),
            V((WIDE, 32, 256), BF16), V((WIDE, 32, 256), BF16),
            V((32, D), F32), V((64, D), F32), V((64, D), F32), V((32, D), F32),
            V((16, 256), F32), V((16, D), F32), V((8, 256), F32),
            sem((8,)), sem((WIDE,)), sem((WIDE,)), sem((WIDE,)), sem((WIDE,)),
            sem((HALF,)), sem((HALF,)), sem((HALF,)), sem((HALF,)), sem((HALF,)), sem((HALF,)),
            sem((3,)), sem((3,)),
        ],
        compiler_params=pltpu.CompilerParams(
            collective_id=0, has_side_effects=True, vmem_limit_bytes=58 * 2**20
        ),
        name="rollout_fork",
    )(
        span_query.reshape(TOK * KHEADS, D), span_key.reshape(TOK * KHEADS, D),
        span_value.reshape(TOK * HEADS, D), span_beta_logit.T, span_logdecay.T,
        span_gate.reshape(TOK * HEADS, D), norm_gain.reshape(1, D), prior_state,
        step_query, step_key, step_value, step_beta_logit, step_logdecay, step_gate,
        rows(cache_key), rows(cache_value), att_query, att_key, att_value, att_gate,
    )
    return pl.pallas_call(
        hand_out,
        out_shape=tuple(jax.ShapeDtypeStruct(x.shape, x.dtype) for x in results),
        in_specs=[vm] * 4,
        out_specs=(vm,) * 4,
        compiler_params=pltpu.CompilerParams(vmem_limit_bytes=8 * 2**20),
        name="hand_out",
    )(*results)


def solution(mesh):
    tok = P(("prompt", "wide"), "tp", None)
    tok2 = P(("prompt", "wide"), "tp")
    stp = P(("prompt", "wide"), None, "tp", None)
    stp2 = P(("prompt", "wide"), None, "tp")
    in_specs = (
        tok, tok, tok, tok2, tok2, tok, P(), P(("prompt", "tp"), None, None),
        stp, stp, stp, stp2, stp2, stp,
        P(("prompt", "wide"), None, None), P(("prompt", "wide"), None, None),
        stp, P(("prompt", "wide"), None, None, None), P(("prompt", "wide"), None, None, None), stp,
    )
    out_specs = (
        P(("prompt", "wide"), "tp"),
        stp2,
        P(("prompt", "wide"), "tp", None, None),
        stp2,
    )
    return jax.shard_map(shards, mesh=mesh, in_specs=in_specs, out_specs=out_specs, check_vma=False)
```
